128 devices in a mesh: dp: 32 (over x, y, core), tensor: 4 (over z).
Axes of the slice: x: 4, y: 4, z: 4, core: 2. Of those that a mesh axis runs over, the one named last changes fastest.
Arguments:
- residual: bfloat16 [512, 7168], P('dp'), may hold values from -6 to 6
- query_latent: bfloat16 [512, 128, 512], P('dp', 'tensor'), may hold values from -64 to 64
- query_rope: bfloat16 [512, 128, 64], P('dp', 'tensor'), may hold values from -6 to 6
- cache_latent: bfloat16 [512, 1024, 512], P('dp'), may hold values from -4 to 4
- cache_rope: bfloat16 [512, 64, 1024], P('dp'), may hold values from -6 to 6
- lengths: int32 [512], P('dp'), may hold values from 256 to 1024, as said below
- value_up: bfloat16 [128, 512, 128], P('tensor'), may hold values from -0.25 to 0.25
- out_proj: bfloat16 [16384, 7168], P('tensor', 'dp'), may hold values from -0.5 to 0.5
- gate_proj: bfloat16 [32, 7168, 1024], P('dp', None, 'tensor'), may hold values from -0.0625 to 0.0625
- up_proj: bfloat16 [32, 7168, 1024], P('dp', None, 'tensor'), may hold values from -0.0625 to 0.0625
- down_proj: bfloat16 [32, 1024, 7168], P('dp', 'tensor'), may hold values from -0.1875 to 0.1875
- groups: int32 [512, 4], P('dp'), may hold values from 0 to 7, as said below
- expert_picks: int32 [512, 8], P('dp'), may hold values from 0 to 15, as said below
- gate_levels: int32 [512, 8], P('dp'), may hold values from 1 to 255
Outputs:
- layer_out: bfloat16 [512, 7168], P('dp')
The draws below stay inside these ranges and needn't reach their ends.
Inputs may be any that keep to these rules, and one draw needn't show every extreme that they name: Row r attends to cache positions 0 to lengths[r] - 1; in every draw some row has length 1024. Each row names 4 different groups; among the rows of one index of dp no group is named by more than 8 rows. `expert_picks`: each row's 8 entries differ, so its experts differ. Among the rows of one index of dp no expert is named by more than 8 rows; in every draw one expert is named by exactly 8 rows of every index of dp.
All inputs are finite; a program needn't handle non-finite values.
Results may differ from the reference program's by a relative error of at most 0.02.
Values may be sent and summed in bfloat16 or wider, within the bound.
No kernel may reach another device: no remote copies, remote signals or barrier semaphores. Data moves between devices by JAX's collectives and lax.ppermute only.
A program may use at most 128 MiB of HBM per device.

```python
import jax
import jax.numpy as jnp
from jax import lax

D = 7168
HEADS = 128
LAT = 512
ROPE = 64
V_HEAD = 128
FF = 1024
TOPK = 8
TOPG = 4
B_DEV = 16
S = 1024
ROWS = 512
EXPERTS = 32
GROUPS = 8
EPG = 4


def draw_query_latent(key, part):
    key = jax.random.fold_in(key, 3)
    base_key = jax.random.fold_in(key, 0)
    values = jax.random.truncated_normal(base_key, -4.0, 4.0, (ROWS, HEADS, LAT), jnp.float32)
    return values.astype(jnp.bfloat16)


def draw_cache_latent(key, part):
    key = jax.random.fold_in(key, 5)
    values = jax.random.truncated_normal(key, -4.0, 4.0, (ROWS, S, LAT), jnp.float32)
    return values.astype(jnp.bfloat16)


def draw_lengths(key, part):
    key = jax.random.fold_in(key, 9)
    draw_key, place_key = jax.random.split(key)
    lengths_drawn = jax.random.randint(draw_key, (ROWS,), S // 4, S + 1)
    longest = jax.random.randint(place_key, (), 0, ROWS)
    return jnp.where(jnp.arange(ROWS) == longest, S, lengths_drawn).astype(jnp.int32)


def draw_routing(key):
    hot_key, perm_key, start_key, order_key, pick_key, shuffle_key = jax.random.split(key, 6)
    hot_expert = jax.random.randint(hot_key, (), 0, EXPERTS)
    hot_group = hot_expert // EPG
    blocks = ROWS // B_DEV
    group_range = jnp.arange(GROUPS, dtype=jnp.int32)
    group_score = jax.random.randint(perm_key, (blocks, GROUPS), 0, 4096) * GROUPS + group_range[None, :]
    group_score = jnp.where(group_range[None, :] == hot_group, -1, group_score)
    ranked = jnp.argsort(group_score, axis=1).astype(jnp.int32)
    layout = jnp.roll(ranked, TOPG - 1, axis=1)
    starts = jax.vmap(lambda block_key: jax.random.permutation(block_key, B_DEV))(jax.random.split(start_key, blocks))
    positions = (starts[:, :, None].astype(jnp.int32) + jnp.arange(TOPG, dtype=jnp.int32)[None, None, :]) % GROUPS
    chosen = jnp.take_along_axis(jnp.broadcast_to(layout[:, None, :], (blocks, B_DEV, GROUPS)), positions, axis=2)
    chosen = chosen.reshape(ROWS, TOPG)
    order_score = jax.random.randint(order_key, (ROWS, TOPG), 0, 4096) * TOPG + jnp.arange(TOPG, dtype=jnp.int32)[None, :]
    groups = jnp.take_along_axis(chosen, jnp.argsort(order_score, axis=1), axis=1)
    present = jnp.any(groups == hot_group, axis=1)
    hot_slot = jnp.argmax(groups == hot_group, axis=1).astype(jnp.int32)
    width_all = TOPG * EPG
    candidate_ids = jnp.arange(width_all, dtype=jnp.int32)
    hot_candidate = hot_slot * EPG + hot_expert % EPG
    pick_score = jax.random.randint(pick_key, (ROWS, width_all), 0, 4096) * width_all + candidate_ids[None, :]
    forced = present[:, None] & (candidate_ids[None, :] == hot_candidate[:, None])
    pick_score = jnp.where(forced, 8192 * width_all, pick_score)
    unused_values, picked = lax.top_k(pick_score, TOPK)
    shuffle_score = jax.random.randint(shuffle_key, (ROWS, TOPK), 0, 4096) * TOPK + jnp.arange(TOPK, dtype=jnp.int32)[None, :]
    expert_picks = jnp.take_along_axis(picked, jnp.argsort(shuffle_score, axis=1), axis=1)
    return (groups.astype(jnp.int32), expert_picks.astype(jnp.int32))


def draw_groups(key, part):
    routed = draw_routing(key)
    return routed[0]


def draw_expert_picks(key, part):
    routed = draw_routing(key)
    return routed[1]


def plant(entries, key, least, largest):
    extent = entries.shape
    spot = [jax.random.randint(jax.random.fold_in(key, axis), (), 0, extent[axis]) for axis in range(len(extent))]
    entries = entries.at[tuple(spot)].set(least)
    longest = extent.index(max(extent))
    spot[longest] = (spot[longest] + 1) % extent[longest]
    return entries.at[tuple(spot)].set(largest)


def steps_of(rng, extent, shards, smallest, high):
    level = 1.0
    for position, shards_of in shards:
        draws = jax.random.uniform(jax.random.fold_in(jax.random.fold_in(rng, 6), position), (shards_of,), jnp.float32, smallest / len(shards), high / len(shards))
        level = level * jnp.repeat(jnp.exp(draws), extent[position] // shards_of).reshape((-1,) + (1,) * (len(extent) - 1 - position))
    return level


def noise(key, dims, deviation, most, pieces=(), held_as=jnp.bfloat16):
    loudness = steps_of(key, dims, pieces, -0.22, 0.18) if pieces else 1.0
    entries = jax.random.normal(key, dims, jnp.float32) * deviation * loudness
    return jnp.minimum(jnp.maximum(entries, -most), most).astype(held_as)


def setup_inputs(seed: int = 0) -> dict:
    seeds = jax.random.split(jax.random.key(seed), 15)
    residual = noise(seeds[0], (ROWS, D), 1.0, 6.0, ((0, 32),))
    query_latent = draw_query_latent(jax.random.fold_in(seeds[14], 71), 0)
    query_rope = noise(seeds[2], (ROWS, HEADS, ROPE), 1.0, 6.0, ((0, 32), (1, 4)))
    cache_latent = draw_cache_latent(jax.random.fold_in(seeds[14], 71), 0)
    cache_rope = noise(seeds[4], (ROWS, ROPE, S), 1.0, 6.0, ((0, 32),))
    lengths = draw_lengths(jax.random.fold_in(seeds[14], 71), 0)
    value_up = noise(seeds[6], (HEADS, LAT, V_HEAD), LAT ** -0.5, 0.25, ((0, 4),))
    out_proj = noise(seeds[7], (HEADS * V_HEAD, D), V_HEAD ** -0.5, 0.5, ((0, 4), (1, 32)))
    gate_proj = noise(seeds[8], (EXPERTS, D, FF), D ** -0.5, 0.0625, ((0, 32), (2, 4)))
    up_proj = noise(seeds[9], (EXPERTS, D, FF), D ** -0.5, 0.0625, ((0, 32), (2, 4)))
    down_proj = noise(seeds[10], (EXPERTS, FF, D), FF ** -0.5, 0.1875, ((0, 32), (1, 4)))
    groups = draw_groups(jax.random.fold_in(seeds[14], 71), 0)
    expert_picks = draw_expert_picks(jax.random.fold_in(seeds[14], 71), 0)
    gate_levels = plant(jax.random.randint(seeds[13], (ROWS, TOPK), 1, 256), jax.random.fold_in(seeds[13], 1), 1, 255).astype(jnp.int32)
    return dict(residual=residual, query_latent=query_latent, query_rope=query_rope, cache_latent=cache_latent, cache_rope=cache_rope, lengths=lengths, value_up=value_up, out_proj=out_proj, gate_proj=gate_proj, up_proj=up_proj, down_proj=down_proj, groups=groups, expert_picks=expert_picks, gate_levels=gate_levels)


score_scale = 192.0 ** -0.5
route_scale = 2.5
far_below = -1.0e30


def attend_row(operands):
    row_query, row_rope, row_cache, row_keys, row_length = operands
    scores = jnp.dot(row_query, row_cache.T, preferred_element_type=jnp.float32)
    scores = (scores + jnp.dot(row_rope, row_keys, preferred_element_type=jnp.float32)) * score_scale
    visible = jnp.arange(S) < row_length
    scores = jnp.where(visible[None, :], scores, far_below)
    highest = jnp.max(scores, axis=1, keepdims=True)
    raised = jnp.exp(scores - highest)
    weights = (raised / jnp.sum(raised, axis=1, keepdims=True)).astype(jnp.bfloat16)
    return jnp.dot(weights, row_cache, preferred_element_type=jnp.float32).astype(jnp.bfloat16)


def reference(residual, query_latent, query_rope, cache_latent, cache_rope, lengths, value_up, out_proj, gate_proj, up_proj, down_proj, groups, expert_picks, gate_levels):
    latent_mix = lax.map(attend_row, (query_latent, query_rope, cache_latent, cache_rope, lengths))
    latent_mix = lax.optimization_barrier(latent_mix)
    head_out = jnp.einsum("rhl,hlv->rhv", latent_mix.astype(jnp.float32), value_up.astype(jnp.float32)).astype(jnp.bfloat16)
    head_out = head_out.reshape(ROWS, HEADS * V_HEAD)
    attention = lax.optimization_barrier(jnp.dot(head_out, out_proj, preferred_element_type=jnp.float32).astype(jnp.bfloat16))
    hidden = (residual.astype(jnp.float32) + attention.astype(jnp.float32)).astype(jnp.bfloat16)
    hidden = lax.optimization_barrier(hidden)
    slot_group = expert_picks // EPG
    expert_ids = jnp.take_along_axis(groups, slot_group, axis=1) * EPG + expert_picks % EPG
    levels = gate_levels.astype(jnp.float32)
    gates = route_scale * levels / jnp.sum(levels, axis=1, keepdims=True)

    def one_expert(running, operands):
        expert_index, gate_weight, up_weight, down_weight = operands
        coefficient = jnp.sum(jnp.where(expert_ids == expert_index, gates, 0.0), axis=1)
        gated = jnp.dot(hidden, gate_weight, preferred_element_type=jnp.float32)
        upward = jnp.dot(hidden, up_weight, preferred_element_type=jnp.float32)
        activation = (jax.nn.silu(gated) * upward).astype(jnp.bfloat16)
        produced = lax.optimization_barrier(jnp.dot(activation, down_weight, preferred_element_type=jnp.float32).astype(jnp.bfloat16))
        return running + coefficient[:, None] * produced.astype(jnp.float32), None

    routed, unused = lax.scan(one_expert, jnp.zeros((ROWS, D), jnp.float32), (jnp.arange(EXPERTS, dtype=jnp.int32), gate_proj, up_proj, down_proj))
    return (hidden.astype(jnp.float32) + routed).astype(jnp.bfloat16)
```

```python
import jax
import jax.numpy as jnp
from jax import lax
from jax.experimental import pallas as pl
from jax.experimental.pallas import tpu as pltpu
from jax.sharding import PartitionSpec as P

SIDE = 4
CORES = 2
CHIPS = SIDE * SIDE
PLANES = 4
TOPG = 4
GROUPS = 8
EPG = 4
CAP = 8

score_scale = 192.0 ** (-0.5)
route_scale = 2.5
far_below = -1e30

f32 = jnp.float32
bf16 = jnp.bfloat16


def dp_index(x, y, c):
    return (x * SIDE + y) * CORES + c


def shift_pairs(dx, dy, dc):
    pairs = []
    for x in range(SIDE):
        for y in range(SIDE):
            for c in range(CORES):
                pairs.append(
                    (dp_index(x, y, c), dp_index((x + dx) % SIDE, (y + dy) % SIDE, (c + dc) % CORES))
                )
    return pairs


def move_x(value, by):
    return lax.ppermute(value, "dp", shift_pairs(by, 0, 0))


def move_y(value, by):
    return lax.ppermute(value, "dp", shift_pairs(0, by, 0))


def move_core(value):
    return lax.ppermute(value, "dp", shift_pairs(0, 0, 1))


def move_z(value, by):
    return lax.ppermute(value, "tensor", [(z, (z + by) % PLANES) for z in range(PLANES)])


def chip_exchange(value):
    groups = [[dp_index(x, y, c) for x in range(SIDE) for y in range(SIDE)] for c in range(CORES)]
    return lax.all_to_all(
        value, "dp", split_axis=0, concat_axis=0, axis_index_groups=groups, tiled=True
    )


ROWS_STEP = 2


def attend_kernel(lengths, q_ref, qr_ref, k_ref, r_ref, vu_hbm, out_ref, mix_ref, vu_ref, sem):
    step = pl.program_id(0)
    copy = pltpu.make_async_copy(vu_hbm, vu_ref, sem)

    @pl.when(step == 0)
    def _():
        copy.start()

    heads = q_ref.shape[1]
    for i in range(ROWS_STEP):
        row = step * ROWS_STEP + i
        keys = k_ref[i]
        scores = lax.dot_general(
            q_ref[i], keys, (((1,), (1,)), ((), ())), preferred_element_type=f32
        )
        scores = scores + jnp.dot(qr_ref[i], r_ref[i], preferred_element_type=f32)
        scores = scores * score_scale
        place = lax.broadcasted_iota(jnp.int32, scores.shape, 1)
        scores = jnp.where(place < lengths[row], scores, far_below)
        highest = jnp.max(scores, axis=1, keepdims=True)
        raised = jnp.exp(scores - highest)
        weights = (raised / jnp.sum(raised, axis=1, keepdims=True)).astype(bf16)
        mix = jnp.dot(weights, keys, preferred_element_type=f32)
        at = pl.ds(pl.multiple_of(row * heads, heads), heads)
        for j in range(mix_ref.shape[0]):
            mix_ref[j, at, :] = mix[:, j * 128 : (j + 1) * 128]

    @pl.when(step == pl.num_programs(0) - 1)
    def _():
        copy.wait()
        rows = out_ref.shape[0]
        width = vu_ref.shape[2]
        for h in range(heads):
            left = [mix_ref[j, pl.ds(h, rows, stride=heads), :] for j in range(mix_ref.shape[0])]
            left = jnp.concatenate(left, axis=1).astype(bf16)
            out_ref[:, h * width : (h + 1) * width] = jnp.dot(
                left, vu_ref[h], preferred_element_type=f32
            ).astype(bf16)


def attend(query_latent, query_rope, cache_latent, cache_rope, lengths, value_up):
    rows, heads, lat = query_latent.shape
    rope = query_rope.shape[2]
    positions = cache_latent.shape[1]
    width = value_up.shape[2]
    return pl.pallas_call(
        attend_kernel,
        grid_spec=pltpu.PrefetchScalarGridSpec(
            num_scalar_prefetch=1,
            grid=(rows // ROWS_STEP,),
            in_specs=[
                pl.BlockSpec((ROWS_STEP, heads, lat), lambda i, n: (i, 0, 0)),
                pl.BlockSpec((ROWS_STEP, heads, rope), lambda i, n: (i, 0, 0)),
                pl.BlockSpec((ROWS_STEP, positions, lat), lambda i, n: (i, 0, 0)),
                pl.BlockSpec((ROWS_STEP, rope, positions), lambda i, n: (i, 0, 0)),
                pl.BlockSpec(memory_space=pl.ANY),
            ],
            out_specs=pl.BlockSpec((rows, heads * width), lambda i, n: (0, 0)),
            scratch_shapes=[
                pltpu.VMEM((lat // 128, rows * heads, 128), f32),
                pltpu.VMEM((heads, lat, width), bf16),
                pltpu.SemaphoreType.DMA,
            ],
        ),
        out_shape=jax.ShapeDtypeStruct((rows, heads * width), bf16),
        compiler_params=pltpu.CompilerParams(vmem_limit_bytes=32 * 1024 * 1024),
        cost_estimate=pl.CostEstimate(
            flops=4 * rows * heads * positions * lat,
            bytes_accessed=2 * rows * positions * (lat + rope),
            transcendentals=rows * heads * positions,
        ),
        name="attend",
    )(lengths, query_latent, query_rope, cache_latent, cache_rope, value_up)


def route_info(groups, expert_picks, gate_levels):
    rows = groups.shape[0]
    group_range = jnp.arange(GROUPS, dtype=jnp.int32)
    member = jnp.any(groups[:, :, None] == group_range[None, None, :], axis=1).astype(jnp.int32)
    below = jnp.arange(rows)[:, None] >= jnp.arange(rows)[None, :]
    counted = jnp.sum(jnp.where(below[:, :, None], member[None, :, :], 0), axis=1)
    place = counted * member
    places = jnp.repeat(place, 16, axis=1)
    slot_range = jnp.arange(TOPG, dtype=jnp.int32)
    picked = jnp.sum(
        jnp.where((expert_picks // EPG)[:, :, None] == slot_range, groups[:, None, :], 0), axis=2
    )
    expert_ids = picked * EPG + expert_picks % EPG
    experts = jnp.arange(GROUPS * EPG, dtype=jnp.int32)
    level = jnp.sum(
        jnp.where(expert_ids[:, :, None] == experts, gate_levels[:, :, None], 0), axis=1
    )
    home = (groups[:, :1] == group_range[None, :]).astype(jnp.int32)
    levels = jnp.concatenate(
        [level, home, jnp.zeros((rows, 128 - GROUPS * EPG - GROUPS), jnp.int32)], axis=1
    )
    return place, places.astype(bf16), levels.astype(bf16)


def select_kernel(table, p0_ref, p1_ref, p2_ref, p3_ref, res_ref, places_ref, out_ref):
    core = table[CHIPS]
    rows = res_ref.shape[2]
    lane = lax.broadcasted_iota(jnp.int32, (2 * rows, 128), 1)
    wanted = (lane % CAP + 1).astype(f32)
    second = lax.broadcasted_iota(jnp.int32, (2 * rows, 128), 0) >= rows
    right_half = (lane % (2 * CAP) >= CAP) == second

    def of(ref, parity, chip):
        return ref[parity ^ core, table[chip]]

    for pair in range(CHIPS // 2):
        for parity in range(CORES):
            parts = []
            marks = []
            for chip in (2 * pair, 2 * pair + 1):
                even = of(p0_ref, parity, chip).astype(f32) + of(p2_ref, parity, chip).astype(f32)
                odd = of(p1_ref, parity, chip).astype(f32) + of(p3_ref, parity, chip).astype(f32)
                attention = (even + odd).astype(bf16).astype(f32)
                parts.append((res_ref[chip, parity].astype(f32) + attention).astype(bf16))
                marks.append(of(places_ref, parity, chip).astype(f32))
            hidden = jnp.concatenate(parts, axis=0)
            mark = jnp.concatenate(marks, axis=0)
            pick = jnp.where((mark == wanted) & right_half, 1.0, 0.0).astype(bf16)
            chosen = lax.dot_general(
                pick, hidden, (((0,), (0,)), ((), ())), preferred_element_type=f32
            ).astype(bf16)
            at = parity * CHIPS * CAP + pair * 2 * CAP
            for group in range(GROUPS):
                block = chosen[group * 2 * CAP : (group + 1) * 2 * CAP]
                out_ref[2 * group, at : at + 2 * CAP, :] = block
                out_ref[2 * group + 1, at : at + 2 * CAP, :] = block


def select(table, parts, residual, places):
    columns = residual.shape[-1]
    slots = CHIPS * CORES * CAP
    whole = pl.BlockSpec(memory_space=pltpu.VMEM)
    return pl.pallas_call(
        select_kernel,
        in_specs=[pl.BlockSpec(memory_space=pltpu.SMEM)] + [whole] * 6,
        out_specs=whole,
        out_shape=jax.ShapeDtypeStruct((CHIPS, slots, columns), bf16),
        compiler_params=pltpu.CompilerParams(vmem_limit_bytes=32 * 1024 * 1024),
        cost_estimate=pl.CostEstimate(flops=10**9, bytes_accessed=6 * 10**6, transcendentals=0),
        name="select",
    )(table, *parts, residual, places)


def up_kernel(scalars, x_ref, gw_ref, uw_ref, *rest):
    if len(rest) == 1:
        (acc_ref,) = rest
        before = None
    else:
        before, acc_ref = rest
    step = pl.program_id(0)

    @pl.when(step == 0)
    def _():
        if before is None:
            acc_ref[...] = jnp.zeros_like(acc_ref)
        else:
            acc_ref[...] = before[...]

    acc_ref[0] += jnp.dot(x_ref[0], gw_ref[0, 0], preferred_element_type=f32)
    acc_ref[1] += jnp.dot(x_ref[0], uw_ref[0, 0], preferred_element_type=f32)


def up(scalars, which, x, gate_weight, up_weight, before=None):
    chips, slots, columns = x.shape
    units = gate_weight.shape[-1]
    weight = pl.BlockSpec((1, 1, columns, units), lambda i, s: (i, s[which], 0, 0))
    acc = pl.BlockSpec((2, slots, units), lambda i, s: (0, 0, 0))
    return pl.pallas_call(
        up_kernel,
        grid_spec=pltpu.PrefetchScalarGridSpec(
            num_scalar_prefetch=1,
            grid=(chips,),
            in_specs=[pl.BlockSpec((1, slots, columns), lambda i, s: (i, 0, 0)), weight, weight]
            + ([] if before is None else [acc]),
            out_specs=acc,
        ),
        out_shape=jax.ShapeDtypeStruct((2, slots, units), f32),
        compiler_params=pltpu.CompilerParams(vmem_limit_bytes=24 * 1024 * 1024),
        cost_estimate=pl.CostEstimate(
            flops=4 * chips * slots * columns * units, bytes_accessed=10**7, transcendentals=0
        ),
        name="up",
    )(scalars, x, gate_weight, up_weight, *([] if before is None else [before]))


def down_kernel(scalars, acc_ref, w_ref, coef_ref, home_ref, own_ref, other_ref, *rest):
    if len(rest) == 2:
        received, out_ref = None, rest[0]
        act_ref = rest[1]
    else:
        received, out_ref, act_ref = rest
    step = pl.program_id(0)

    @pl.when(step == 0)
    def _():
        gated = acc_ref[0]
        act_ref[...] = (gated / (1.0 + jnp.exp(-gated)) * acc_ref[1]).astype(bf16)

    produced = jnp.dot(act_ref[...], w_ref[...], preferred_element_type=f32) * coef_ref[...]
    core = scalars[0]
    parts = []
    for chip in range(own_ref.shape[0]):
        mine = own_ref[chip].astype(f32)
        theirs = other_ref[chip].astype(f32)
        flip = core == 1
        parts.append(jnp.where(flip, theirs, mine))
        parts.append(jnp.where(flip, mine, theirs))
    hidden = jnp.concatenate(parts, axis=1)
    produced = produced + hidden * home_ref[...]
    if received is not None:
        produced = produced + received[...].astype(f32)
    out_ref[...] = produced.astype(bf16)


def down(scalars, which, acc, down_weight, coef, home, own, other, received=None):
    units, width = down_weight.shape
    chips, slots, columns = own.shape
    half = slots // CORES
    chips_step = 2
    block = chips_step * CORES * columns
    x_spec = pl.BlockSpec((chips_step, half, columns), lambda i, s: (i, s[which], 0))
    out_spec = pl.BlockSpec((half, block), lambda i, s: (0, i))
    column = pl.BlockSpec((half, 1), lambda i, s: (s[which], 0))
    return pl.pallas_call(
        down_kernel,
        grid_spec=pltpu.PrefetchScalarGridSpec(
            num_scalar_prefetch=1,
            grid=(width // block,),
            in_specs=[
                pl.BlockSpec((2, half, units), lambda i, s: (0, s[which], 0)),
                pl.BlockSpec((units, block), lambda i, s: (0, i)),
                column,
                column,
                x_spec,
                x_spec,
            ]
            + ([] if received is None else [out_spec]),
            out_specs=out_spec,
            scratch_shapes=[pltpu.VMEM((half, units), bf16)],
        ),
        out_shape=jax.ShapeDtypeStruct((half, width), bf16),
        compiler_params=pltpu.CompilerParams(vmem_limit_bytes=24 * 1024 * 1024),
        cost_estimate=pl.CostEstimate(
            flops=2 * half * units * width, bytes_accessed=8 * 10**6, transcendentals=half * units
        ),
        name="down",
    )(scalars, acc, down_weight, coef, home, own, other, *([] if received is None else [received]))


def around(value, move):
    return jnp.stack([value, move(value, 1), move(value, 3), move(value, 2)])


ORDER = (0, 1, 3, 2)


def local(
    residual,
    query_latent,
    query_rope,
    cache_latent,
    cache_rope,
    lengths,
    value_up,
    out_proj,
    gate_proj,
    up_proj,
    down_proj,
    groups,
    expert_picks,
    gate_levels,
):
    rows, model = residual.shape
    columns = out_proj.shape[1]
    dp = lax.axis_index("dp")
    z = lax.axis_index("tensor")
    core = dp % CORES
    chip = dp // CORES
    here_x, here_y = chip // SIDE, chip % SIDE

    spread = residual.reshape(rows, CHIPS * CORES, columns).transpose(1, 0, 2)
    residual_columns = lax.all_to_all(spread, "dp", split_axis=0, concat_axis=0, tiled=True)
    residual_columns = residual_columns.reshape(CHIPS, CORES, rows, columns)

    place, places, levels = route_info(groups, expert_picks, gate_levels)
    head_out = attend(query_latent, query_rope, cache_latent, cache_rope, lengths, value_up)

    half = head_out.shape[1] // 2
    first = jnp.concatenate([head_out[:, :half], places], axis=1)
    second = jnp.concatenate([head_out[:, half:], levels], axis=1)
    first = around(around(first, move_x), move_y)
    second = around(around(second, move_y), move_x)
    wide = half + 128
    first = first.reshape(CHIPS * rows, wide)
    second = second.reshape(CHIPS * rows, wide)
    first_other = move_core(first)
    second_other = move_core(second)

    def project(block, weight):
        return jnp.dot(block[:, :half], weight, preferred_element_type=f32)

    def terms(one, two):
        a = project(one, out_proj[:half]).reshape(SIDE, SIDE, rows, columns)
        b = project(two, out_proj[half:]).reshape(SIDE, SIDE, rows, columns)
        return (a + b.transpose(1, 0, 2, 3)).astype(bf16).reshape(CHIPS, rows, columns)

    partial = jnp.stack([terms(first, second), terms(first_other, second_other)])
    parts = [partial, move_z(partial, 1), move_z(partial, 2), move_z(partial, 3)]

    spot = jnp.array([ORDER.index(k) for k in range(SIDE)], jnp.int32)
    far = jnp.arange(SIDE, dtype=jnp.int32)
    x_spot = jnp.take(spot, (here_x - far) % SIDE)
    y_spot = jnp.take(spot, (here_y - far) % SIDE)
    first_place = (y_spot[None, :] * SIDE + x_spot[:, None]).reshape(CHIPS)
    second_place = (x_spot[:, None] * SIDE + y_spot[None, :]).reshape(CHIPS)
    table = jnp.concatenate([first_place, core[None]]).astype(jnp.int32)

    places_all = jnp.stack([first[:, half:], first_other[:, half:]]).reshape(CORES, CHIPS, rows, 128)
    outgoing = select(table, parts, residual_columns, places_all)
    own = chip_exchange(outgoing)
    other = move_core(own)

    group = dp // EPG
    levels_all = jnp.stack([second[:, half:], second_other[:, half:]]).astype(f32)
    levels_all = levels_all.reshape(CORES, CHIPS, rows, 128)
    marks = places_all.astype(f32)

    def in_order(value, at):
        to = (jnp.arange(CHIPS)[None, :] == at[:, None]).astype(f32)
        value = jnp.einsum("ap,cpr->car", to, value, precision=lax.Precision.HIGHEST)
        return jnp.where(core == 0, value, value[::-1])

    sums = jnp.sum(levels_all[..., : GROUPS * EPG], axis=-1)
    mine = lax.dynamic_index_in_dim(levels_all, dp, 3, keepdims=False)
    gates = in_order(route_scale * mine / sums, second_place)
    homes = in_order(
        lax.dynamic_index_in_dim(levels_all, GROUPS * EPG + group, 3, keepdims=False), second_place
    )
    ranks = in_order(lax.dynamic_index_in_dim(marks, group * 16, 3, keepdims=False), first_place)
    hits = ranks[..., None, :] == jnp.arange(1, CAP + 1, dtype=f32)[:, None]
    slots = CORES * CHIPS * CAP
    coef = jnp.sum(jnp.where(hits, gates[..., None, :], 0.0), axis=-1).reshape(slots, 1)
    first_chip = (z == 0) & (dp % EPG == 0)
    home = jnp.sum(jnp.where(hits, homes[..., None, :], 0.0), axis=-1).reshape(slots, 1)
    home = jnp.where(first_chip, home, 0.0)

    gate_weight = gate_proj.reshape(CHIPS, CORES, columns, -1)
    up_weight = up_proj.reshape(CHIPS, CORES, columns, -1)
    scalars = jnp.stack([core, 1 - core]).astype(jnp.int32)
    acc = up(scalars, 0, own, gate_weight, up_weight)
    acc = up(scalars, 1, other, gate_weight, up_weight, acc)
    for_other = down(scalars, 1, acc, down_proj[0], coef, home, own, other)
    returning = down(scalars, 0, acc, down_proj[0], coef, home, own, other, move_core(for_other))

    returned = chip_exchange(returning.reshape(CHIPS, CAP, model)).reshape(CHIPS * CAP, model)
    slot = jnp.arange(1, CAP + 1, dtype=jnp.int32)
    weighting = jnp.repeat(place, 2, axis=1)[:, :, None] == slot[None, None, :]
    weighting = weighting.astype(bf16).reshape(rows, CHIPS * CAP)
    mixed = jnp.dot(weighting, returned, preferred_element_type=f32).astype(bf16)
    even = mixed.astype(f32) + move_z(mixed, 2).astype(f32)
    odd = move_z(mixed, 1).astype(f32) + move_z(mixed, 3).astype(f32)
    return (even + odd).astype(bf16)


def solution(mesh):
    return jax.shard_map(
        local,
        mesh=mesh,
        in_specs=(
            P("dp", None),
            P("dp", "tensor", None),
            P("dp", "tensor", None),
            P("dp", None, None),
            P("dp", None, None),
            P("dp"),
            P("tensor", None, None),
            P("tensor", "dp"),
            P("dp", None, "tensor"),
            P("dp", None, "tensor"),
            P("dp", "tensor", None),
            P("dp", None),
            P("dp", None),
            P("dp", None),
        ),
        out_specs=P("dp", None),
        check_vma=False,
    )
```

```python
import jax
import jax.numpy as jnp
from jax import lax
from jax.experimental import pallas as pl
from jax.experimental.pallas import tpu as pltpu
from jax.sharding import PartitionSpec as P

SIDE = 4
CORES = 2
CHIPS = SIDE * SIDE
PLANES = 4
TOPG = 4
GROUPS = 8
EPG = 4
CAP = 8
QUARTER = 4
PART = QUARTER * CAP

score_scale = 192.0 ** (-0.5)
route_scale = 2.5
far_below = -1e30

f32 = jnp.float32
bf16 = jnp.bfloat16
VMEM = 28 * 1024 * 1024


def distant(value):
    return pltpu.with_memory_space_constraint(value, pltpu.HBM)


def dp_index(x, y, c):
    return (x * SIDE + y) * CORES + c


def place_pairs(place):
    return [
        (dp_index(x, y, c), dp_index(*place(x, y, c)))
        for x in range(SIDE)
        for y in range(SIDE)
        for c in range(CORES)
    ]


def move_core(value):
    return lax.ppermute(value, "dp", place_pairs(lambda x, y, c: (x, y, 1 - c)))


def move_ring(value, by, x_core):
    def place(x, y, c):
        return ((x + by) % SIDE, y, c) if c == x_core else (x, (y + by) % SIDE, c)

    return lax.ppermute(value, "dp", place_pairs(place))


def move_z(value, by):
    return lax.ppermute(value, "tensor", [(z, (z + by) % PLANES) for z in range(PLANES)])


def sum_z(low, high):
    def add(block, mask):
        pairs = [(z, z ^ mask) for z in range(PLANES)]
        moved = lax.ppermute(block, "tensor", pairs)
        return (block.astype(f32) + moved.astype(f32)).astype(bf16)

    low, high = add(low, 1), add(high, 3)
    low, high = add(low, 3), add(high, 1)
    return low, high


def chip_exchange(value):
    groups = [[dp_index(x, y, c) for x in range(SIDE) for y in range(SIDE)] for c in range(CORES)]
    return lax.all_to_all(
        value, "dp", split_axis=0, concat_axis=0, axis_index_groups=groups, tiled=True
    )


CHUNK = 256
DEPTH = 6


def this_core():
    return lax.axis_index("dp") % CORES


def upright(ref):
    rows = ref.shape[1]
    same = lax.broadcasted_iota(jnp.int32, (rows, rows), 0) == lax.broadcasted_iota(
        jnp.int32, (rows, rows), 1
    )
    turned = lax.dot_general(
        jnp.where(same, 1.0, 0.0).astype(bf16),
        ref[...].astype(f32).astype(bf16),
        (((1,), (1,)), ((), ())),
        preferred_element_type=f32,
    )
    return turned.astype(jnp.int32)


def route_tables(groups, picks, levels):
    rows = groups.shape[0]
    lane = lax.broadcasted_iota(jnp.int32, (rows, 128), 1)
    member = lane < 0
    for t in range(TOPG):
        member = member | (lane // 16 == groups[:, t : t + 1])
    below = lax.broadcasted_iota(jnp.int32, (rows, rows), 0) >= lax.broadcasted_iota(
        jnp.int32, (rows, rows), 1
    )
    counted = jnp.dot(
        jnp.where(below, 1.0, 0.0).astype(bf16),
        jnp.where(member, 1.0, 0.0).astype(bf16),
        preferred_element_type=f32,
    )
    places = jnp.where(member, counted, 0.0)
    table = jnp.where(lane - GROUPS * EPG == groups[:, :1], 1, 0)
    for k in range(picks.shape[1]):
        pick = picks[:, k : k + 1]
        group = jnp.zeros_like(pick)
        for t in range(TOPG):
            group = jnp.where(pick // EPG == t, groups[:, t : t + 1], group)
        table = jnp.where(lane == group * EPG + pick % EPG, levels[:, k : k + 1], table)
    return places.astype(bf16), table.astype(f32).astype(bf16)


def attend_kernel(
    lengths, q_ref, qr_ref, k_hbm, r_hbm, vu_hbm, groups_ref, picks_ref, levels_ref,
    kept_ref, given_ref, places_ref, k_ref, r_ref, mix_ref, vu_ref, k_sems, r_sems, vu_sem,
):
    rows, heads, lat = q_ref.shape
    positions = k_hbm.shape[1]
    chunks = positions // CHUNK
    width = vu_ref.shape[2]
    core = this_core()
    vu_copy = pltpu.make_async_copy(vu_hbm, vu_ref, vu_sem)

    def held(row):
        return (lengths[row] + CHUNK - 1) // CHUNK

    def copies(row, slot, chunk):
        at = pl.ds(chunk * CHUNK, CHUNK)
        return (
            pltpu.make_async_copy(
                k_hbm.at[row, at, :], k_ref.at[slot, at, :], k_sems.at[slot, chunk]
            ),
            pltpu.make_async_copy(
                r_hbm.at[row, :, at], r_ref.at[slot, :, at], r_sems.at[slot, chunk]
            ),
        )

    def each(row, slot, act):
        for chunk in range(chunks):

            @pl.when(chunk < held(row))
            def _():
                for copy in copies(row, slot, chunk):
                    act(copy)

    for row in range(DEPTH):
        each(row, row, lambda copy: copy.start())
    vu_copy.start()

    places, levels = route_tables(upright(groups_ref), upright(picks_ref), upright(levels_ref))
    places_ref[...] = places
    half = heads * width // 2
    first = core == 0
    kept_ref[:, half:] = jnp.where(first, places.astype(f32), levels.astype(f32)).astype(bf16)
    given_ref[:, half:] = jnp.where(first, levels.astype(f32), places.astype(f32)).astype(bf16)

    def step(row, carry):
        slot = lax.rem(row, DEPTH)
        each(row, slot, lambda copy: copy.wait())
        for count in range(1, chunks + 1):

            @pl.when(held(row) == count)
            def _():
                seen = count * CHUNK
                keys = k_ref[slot, :seen, :]
                scores = lax.dot_general(
                    q_ref[row], keys, (((1,), (1,)), ((), ())), preferred_element_type=f32
                )
                scores = scores + jnp.dot(
                    qr_ref[row], r_ref[slot, :, :seen], preferred_element_type=f32
                )
                scores = scores * score_scale
                place = lax.broadcasted_iota(jnp.int32, scores.shape, 1)
                scores = jnp.where(place < lengths[row], scores, far_below)
                highest = jnp.max(scores, axis=1, keepdims=True)
                raised = jnp.exp(scores - highest)
                weights = (raised / jnp.sum(raised, axis=1, keepdims=True)).astype(bf16)
                mix = jnp.dot(weights, keys, preferred_element_type=f32)
                at = pl.ds(pl.multiple_of(row * heads, heads), heads)
                for j in range(mix_ref.shape[0]):
                    mix_ref[j, at, :] = mix[:, j * 128 : (j + 1) * 128]

        @pl.when(row + DEPTH < rows)
        def _():
            each(row + DEPTH, slot, lambda copy: copy.start())

        return carry

    lax.fori_loop(0, rows, step, 0)
    vu_copy.wait()
    for side, ref in ((core, kept_ref), (1 - core, given_ref)):
        for i in range(heads // 2):
            h = side * (heads // 2) + i
            left = [mix_ref[j, pl.ds(h, rows, stride=heads), :] for j in range(mix_ref.shape[0])]
            left = jnp.concatenate(left, axis=1).astype(bf16)
            ref[:, i * width : (i + 1) * width] = jnp.dot(
                left, vu_ref[h], preferred_element_type=f32
            ).astype(bf16)


def attend(query_latent, query_rope, cache_latent, cache_rope, lengths, value_up, routing):
    rows, heads, lat = query_latent.shape
    rope = query_rope.shape[2]
    positions = cache_latent.shape[1]
    width = value_up.shape[2]
    whole = pl.BlockSpec(memory_space=pltpu.VMEM)
    small = pl.BlockSpec(memory_space=pltpu.SMEM)
    far = pl.BlockSpec(memory_space=pltpu.HBM)
    return pl.pallas_call(
        attend_kernel,
        in_specs=[small, whole, whole, far, far, far, whole, whole, whole],
        out_specs=(whole,) * 3,
        out_shape=(
            jax.ShapeDtypeStruct((rows, heads * width // 2 + 128), bf16),
            jax.ShapeDtypeStruct((rows, heads * width // 2 + 128), bf16),
            jax.ShapeDtypeStruct((rows, 128), bf16),
        ),
        scratch_shapes=[
            pltpu.VMEM((DEPTH, positions, lat), bf16),
            pltpu.VMEM((DEPTH, rope, positions), bf16),
            pltpu.VMEM((lat // 128, rows * heads, 128), f32),
            pltpu.VMEM((heads, lat, width), bf16),
            pltpu.SemaphoreType.DMA((DEPTH, positions // CHUNK)),
            pltpu.SemaphoreType.DMA((DEPTH, positions // CHUNK)),
            pltpu.SemaphoreType.DMA,
        ],
        compiler_params=pltpu.CompilerParams(vmem_limit_bytes=VMEM),
        cost_estimate=pl.CostEstimate(
            flops=4 * rows * heads * positions * lat,
            bytes_accessed=2 * rows * positions * (lat + rope),
            transcendentals=rows * heads * positions,
        ),
        name="attend",
    )(
        lengths, query_latent, query_rope, distant(cache_latent), distant(cache_rope), distant(value_up),
        *routing,
    )


def project_kernel(*refs):
    count = 2 * SIDE
    blocks_hbm, w_hbm = refs[:count], refs[count]
    low_ref, high_ref, places_ref, levels_ref = refs[count + 1 : count + 5]
    b_ref, w_ref, b_sems, w_sems = refs[count + 5 :]
    core = this_core()
    half = w_ref.shape[2]
    lanes = [pl.ds(pl.multiple_of(side * half, half), half) for side in (core, 1 - core)]
    w_copies = [
        pltpu.make_async_copy(w_hbm.at[:, lanes[n]], w_ref.at[n], w_sems.at[n]) for n in range(2)
    ]
    copies = [
        pltpu.make_async_copy(blocks_hbm[n], b_ref.at[n], b_sems.at[n]) for n in range(count)
    ]
    w_copies[0].start()
    for copy in copies[:SIDE]:
        copy.start()
    w_copies[1].start()
    for copy in copies[SIDE:]:
        copy.start()
    made = []
    for n in range(count):
        if n % SIDE == 0:
            w_copies[n // SIDE].wait()
        copies[n].wait()
        made.append(
            lax.dot_general(
                b_ref[n, :, :half], w_ref[n // SIDE], (((1,), (1,)), ((), ())),
                preferred_element_type=f32,
            )
        )
    rows = made[0].shape[0] // SIDE
    first = core == 0
    for i in range(SIDE):
        for j in range(SIDE):
            at, across = slice(j * rows, (j + 1) * rows), slice(i * rows, (i + 1) * rows)
            total = (made[i][at] + made[SIDE + j][across]).astype(bf16)
            (low_ref if i < 2 else high_ref)[i % 2 * SIDE + j] = total
            mine = b_ref[i, at, half:].astype(f32)
            theirs = b_ref[SIDE + j, across, half:].astype(f32)
            places_ref[i * SIDE + j] = jnp.where(first, mine, theirs).astype(bf16)
            levels_ref[i * SIDE + j] = jnp.where(first, theirs, mine).astype(bf16)


def project(blocks, swapped, out_proj):
    wide = blocks[0].shape[1]
    rows = blocks[0].shape[0] // SIDE
    columns = out_proj.shape[1]
    whole = pl.BlockSpec(memory_space=pltpu.VMEM)
    far = pl.BlockSpec(memory_space=pltpu.HBM)
    sums = jax.ShapeDtypeStruct((CHIPS // 2, rows, columns), bf16)
    table = jax.ShapeDtypeStruct((CHIPS, rows, 128), bf16)
    return pl.pallas_call(
        project_kernel,
        in_specs=[far] * (2 * SIDE + 1),
        out_specs=(whole,) * 4,
        out_shape=(sums, sums, table, table),
        scratch_shapes=[
            pltpu.VMEM((2 * SIDE, SIDE * rows, wide), bf16),
            pltpu.VMEM((2, columns, out_proj.shape[0] // 2), bf16),
            pltpu.SemaphoreType.DMA((2 * SIDE,)),
            pltpu.SemaphoreType.DMA((2,)),
        ],
        compiler_params=pltpu.CompilerParams(vmem_limit_bytes=VMEM),
        cost_estimate=pl.CostEstimate(flops=10**9, bytes_accessed=7 * 10**6, transcendentals=0),
        name="project",
    )(*blocks, *swapped, distant(out_proj.T))


def slot_masks(mark, rows):
    lane = lax.broadcasted_iota(jnp.int32, (2 * rows, 128), 1)
    wanted = (lane % CAP + 1).astype(f32)
    second = lax.broadcasted_iota(jnp.int32, (2 * rows, 128), 0) >= rows
    right_half = (lane % (2 * CAP) >= CAP) == second
    return jnp.where((mark == wanted) & right_half, 1.0, 0.0).astype(bf16)


def gate_kernel(table, places_ref, levels_ref, out_ref, made_ref):
    dp = lax.axis_index("dp")
    group = dp // EPG
    rows = places_ref.shape[1] // CORES
    lane = lax.broadcasted_iota(jnp.int32, (2 * rows, 128), 1)
    for quarter in range(CHIPS // QUARTER):
        for parity in range(CORES):
            for pair in range(QUARTER // 2):
                chips = (quarter * QUARTER + 2 * pair, quarter * QUARTER + 2 * pair + 1)
                at = slice(parity * rows, (parity + 1) * rows)
                mark = jnp.concatenate([places_ref[table[chip], at].astype(f32) for chip in chips])
                level = jnp.concatenate([levels_ref[table[chip], at].astype(f32) for chip in chips])
                total = jnp.sum(jnp.where(lane < GROUPS * EPG, level, 0.0), axis=1, keepdims=True)
                mine = jnp.sum(jnp.where(lane == dp, level, 0.0), axis=1, keepdims=True)
                home = jnp.sum(
                    jnp.where(lane == GROUPS * EPG + group, level, 0.0), axis=1, keepdims=True
                )
                gate = route_scale * mine / total
                high = gate.astype(bf16).astype(f32)
                values = jnp.where(lane == 0, high, jnp.where(lane == 1, gate - high, 0.0))
                values = jnp.where(lane == 2, home, values).astype(bf16)
                made_ref[...] = lax.dot_general(
                    slot_masks(mark, rows), values, (((0,), (0,)), ((), ())),
                    preferred_element_type=f32,
                )
                to = quarter * CORES * PART + parity * PART + pair * 2 * CAP
                out_ref[to : to + 2 * CAP] = made_ref[
                    pl.ds(pl.multiple_of(group * 2 * CAP, 2 * CAP), 2 * CAP)
                ]


def gate_table(table, places, levels):
    whole = pl.BlockSpec(memory_space=pltpu.VMEM)
    return pl.pallas_call(
        gate_kernel,
        in_specs=[pl.BlockSpec(memory_space=pltpu.SMEM), whole, whole],
        out_specs=whole,
        out_shape=jax.ShapeDtypeStruct((CHIPS * CORES * CAP, 128), f32),
        scratch_shapes=[pltpu.VMEM((128, 128), f32)],
        compiler_params=pltpu.CompilerParams(vmem_limit_bytes=VMEM),
        cost_estimate=pl.CostEstimate(flops=10**8, bytes_accessed=10**6, transcendentals=0),
        name="gate_table",
    )(table, places, levels)


def select_kernel(table, low_ref, high_ref, res_ref, places_ref, out_ref):
    rows = res_ref.shape[2]

    def attention_of(parity, chip):
        place = table[chip]
        side = CHIPS // 2
        inside = place % side
        at = slice(parity * rows, (parity + 1) * rows)
        return jnp.where(place < side, low_ref[inside, at].astype(f32), high_ref[inside, at].astype(f32))

    for parity in range(CORES):
        for pair in range(QUARTER // 2):
            quarters = []
            for quarter in range(CHIPS // QUARTER):
                parts = []
                marks = []
                for chip in (quarter * QUARTER + 2 * pair, quarter * QUARTER + 2 * pair + 1):
                    attention = attention_of(parity, chip)
                    parts.append((res_ref[chip, parity].astype(f32) + attention).astype(bf16))
                    at = slice(parity * rows, (parity + 1) * rows)
                    marks.append(places_ref[table[chip], at].astype(f32))
                hidden = jnp.concatenate(parts, axis=0)
                mark = jnp.concatenate(marks, axis=0)
                pick = slot_masks(mark, rows)
                quarters.append(
                    lax.dot_general(
                        pick, hidden, (((0,), (0,)), ((), ())), preferred_element_type=f32
                    )
                )
            chosen = jnp.concatenate(quarters, axis=1).astype(bf16)
            at = parity * PART + pair * 2 * CAP
            for group in range(GROUPS):
                block = chosen[group * 2 * CAP : (group + 1) * 2 * CAP]
                out_ref[2 * group, at : at + 2 * CAP, :] = block
                out_ref[2 * group + 1, at : at + 2 * CAP, :] = block


def select(table, parts, residual, places):
    columns = residual.shape[-1]
    whole = pl.BlockSpec(memory_space=pltpu.VMEM)
    return pl.pallas_call(
        select_kernel,
        in_specs=[pl.BlockSpec(memory_space=pltpu.SMEM)] + [whole] * 4,
        out_specs=whole,
        out_shape=jax.ShapeDtypeStruct(
            (CHIPS, CORES * PART, CHIPS // QUARTER * columns), bf16
        ),
        compiler_params=pltpu.CompilerParams(vmem_limit_bytes=VMEM),
        cost_estimate=pl.CostEstimate(flops=10**9, bytes_accessed=6 * 10**6, transcendentals=0),
        name="select",
    )(table, *parts, residual, places)


def unpacked(block, columns):
    parts = [block[:, q * columns : (q + 1) * columns] for q in range(CHIPS // QUARTER)]
    return jnp.concatenate(parts, axis=0)


def raise_up(x_ref, gw_hbm, uw_hbm, w_ref, sems, core, acc):
    columns, units = gw_hbm.shape[2:]
    span = CHIPS // QUARTER
    copies = []
    for part in range(QUARTER):
        chips = pl.ds(part * span, span)
        for n, source in enumerate((gw_hbm, uw_hbm)):
            lanes = slice(n * units, (n + 1) * units)
            copies.append(
                pltpu.make_async_copy(
                    source.at[chips, core], w_ref.at[chips, :, lanes], sems.at[part, n]
                )
            )
    for copy in copies:
        copy.start()
    for chip in range(CHIPS):
        if chip % span == 0:
            copies[chip // span * 2].wait()
            copies[chip // span * 2 + 1].wait()
        acc = acc + jnp.dot(unpacked(x_ref[chip], columns), w_ref[chip], preferred_element_type=f32)
    return acc


def up_kernel(x_ref, gw_hbm, uw_hbm, acc_ref, w_ref, sems):
    zero = jnp.zeros(acc_ref.shape, f32)
    acc_ref[...] = raise_up(x_ref, gw_hbm, uw_hbm, w_ref, sems, this_core(), zero)


def act_kernel(acc_ref, x_ref, gw_hbm, uw_hbm, act_ref, w_ref, sems):
    acc = raise_up(x_ref, gw_hbm, uw_hbm, w_ref, sems, 1 - this_core(), acc_ref[...])
    units = acc.shape[1] // 2
    gated = acc[:, :units]
    act_ref[...] = (gated / (1.0 + jnp.exp(-gated)) * acc[:, units:]).astype(bf16)


def up(x, gate_weight, up_weight, before=None):
    columns, units = gate_weight.shape[2:]
    slots = x.shape[1] * CHIPS // QUARTER
    whole = pl.BlockSpec(memory_space=pltpu.VMEM)
    far = pl.BlockSpec(memory_space=pltpu.HBM)
    operands = (x,) if before is None else (before, x)
    return pl.pallas_call(
        up_kernel if before is None else act_kernel,
        in_specs=[whole] * len(operands) + [far, far],
        out_specs=whole,
        out_shape=(
            jax.ShapeDtypeStruct((slots, 2 * units), f32)
            if before is None
            else jax.ShapeDtypeStruct((slots, units), bf16)
        ),
        scratch_shapes=[
            pltpu.VMEM((CHIPS, columns, 2 * units), bf16),
            pltpu.SemaphoreType.DMA((QUARTER, 2)),
        ],
        compiler_params=pltpu.CompilerParams(vmem_limit_bytes=VMEM),
        cost_estimate=pl.CostEstimate(
            flops=4 * CHIPS * slots * columns * units, bytes_accessed=6 * 10**6, transcendentals=0
        ),
        name="up",
    )(*operands, distant(gate_weight), distant(up_weight))


def cut_kernel(w_hbm, *refs):
    outs, held, sems = refs[:3], refs[3], refs[4]
    z = lax.axis_index("tensor")
    width = outs[0].shape[1]
    copies = []
    for n, by in enumerate((1, 3, 2)):
        lanes = pl.ds(pl.multiple_of((z + by) % PLANES * width, width), width)
        copies.append(pltpu.make_async_copy(w_hbm.at[:, lanes], held.at[n], sems.at[0, n]))
    for copy in copies:
        copy.start()
    leaving = []
    for n, copy in enumerate(copies):
        copy.wait()
        leaving.append(pltpu.make_async_copy(held.at[n], outs[n], sems.at[1, n]))
        leaving[n].start()
    for copy in leaving:
        copy.wait()


def cut(down_weight):
    units, width = down_weight.shape
    far = pl.BlockSpec(memory_space=pltpu.HBM)
    return pl.pallas_call(
        cut_kernel,
        in_specs=[far],
        out_specs=(far,) * 3,
        out_shape=(jax.ShapeDtypeStruct((units, width // PLANES), bf16),) * 3,
        scratch_shapes=[
            pltpu.VMEM((3, units, width // PLANES), bf16),
            pltpu.SemaphoreType.DMA((2, 3)),
        ],
        compiler_params=pltpu.CompilerParams(vmem_limit_bytes=VMEM),
        cost_estimate=pl.CostEstimate(flops=0, bytes_accessed=6 * 10**6, transcendentals=0),
        name="cut",
    )(distant(down_weight))


def down_kernel(a0, a1, a2, a3, own_hbm, w1, w2, w3, gates_ref, out_ref, w_ref, sems):
    acts = (a0, a1, a2, a3)
    z = lax.axis_index("tensor")
    units = a0.shape[1]
    width = out_ref.shape[1]
    lanes = pl.ds(pl.multiple_of(z * width, width), width)
    copies = [
        pltpu.make_async_copy(source, w_ref.at[n * units : (n + 1) * units], sems.at[n])
        for n, source in enumerate((own_hbm.at[:, lanes], w1, w2, w3))
    ]
    for copy in copies:
        copy.start()
    gate = gates_ref[:, 0:1] + gates_ref[:, 1:2]
    left = jnp.concatenate([act[...] for act in acts], axis=1)
    for copy in copies:
        copy.wait()
    block = 256
    for at in range(0, width, block):
        made = jnp.dot(left, w_ref[:, at : at + block], preferred_element_type=f32)
        out_ref[:, at : at + block] = (made * gate).astype(bf16)


def down(acts, own_weight, weights, gates):
    slots = acts[0].shape[0]
    units, width = weights[0].shape
    whole = pl.BlockSpec(memory_space=pltpu.VMEM)
    far = pl.BlockSpec(memory_space=pltpu.HBM)
    return pl.pallas_call(
        down_kernel,
        in_specs=[whole] * 4 + [far] * 4 + [whole],
        out_specs=whole,
        out_shape=jax.ShapeDtypeStruct((slots, width), bf16),
        scratch_shapes=[
            pltpu.VMEM((PLANES * units, width), bf16),
            pltpu.SemaphoreType.DMA((PLANES,)),
        ],
        compiler_params=pltpu.CompilerParams(vmem_limit_bytes=VMEM),
        cost_estimate=pl.CostEstimate(
            flops=8 * slots * units * width, bytes_accessed=6 * 10**6, transcendentals=0
        ),
        name="down",
    )(*acts, distant(own_weight), *[distant(weight) for weight in weights], gates)


def join_kernel(y_ref, received_ref, own_hbm, other_hbm, gates_ref, out_ref, x_ref, sems):
    half, width = out_ref.shape
    columns = own_hbm.shape[2] // (CHIPS // QUARTER)
    dp, z = lax.axis_index("dp"), lax.axis_index("tensor")
    core = dp % CORES
    step_here = dp // CORES % 2
    chips = QUARTER // 2
    near = pl.ds(z * QUARTER + step_here * chips, chips)
    rows = pl.ds(pl.multiple_of(core * PART, PART), PART)
    copies = [
        pltpu.make_async_copy(source.at[near, rows], x_ref.at[n], sems.at[n])
        for n, source in enumerate((own_hbm, other_hbm))
    ]
    for copy in copies:
        copy.start()
    both, homes = [], []
    for q in range(CHIPS // QUARTER):
        at = pl.ds(pl.multiple_of(q * CORES * PART + core * PART, PART), PART)
        both.append(y_ref[at, :].astype(f32) + received_ref[q * PART : (q + 1) * PART, :].astype(f32))
        homes.append(gates_ref[at, 2:3])
    total = jnp.concatenate(both, axis=0)
    home = jnp.concatenate(homes, axis=0)
    out_ref[...] = total.astype(bf16)
    for copy in copies:
        copy.wait()
    block = chips * CORES * columns
    flip = core == 1
    parts = []
    for chip in range(chips):
        mine = unpacked(x_ref[0, chip].astype(f32), columns)
        theirs = unpacked(x_ref[1, chip].astype(f32), columns)
        parts.append(jnp.where(flip, theirs, mine))
        parts.append(jnp.where(flip, mine, theirs))
    hidden = jnp.concatenate(parts, axis=1) * home
    for step in range(width // block):

        @pl.when(step_here == step)
        def _():
            at = slice(step * block, (step + 1) * block)
            out_ref[:, at] = (total[:, at] + hidden).astype(bf16)


def join(y, received, own, other, gates):
    whole = pl.BlockSpec(memory_space=pltpu.VMEM)
    far = pl.BlockSpec(memory_space=pltpu.HBM)
    return pl.pallas_call(
        join_kernel,
        in_specs=[whole, whole, far, far, whole],
        out_specs=whole,
        out_shape=jax.ShapeDtypeStruct(received.shape, bf16),
        scratch_shapes=[
            pltpu.VMEM((2, QUARTER // 2, PART, own.shape[2]), bf16),
            pltpu.SemaphoreType.DMA((2,)),
        ],
        compiler_params=pltpu.CompilerParams(vmem_limit_bytes=VMEM),
        cost_estimate=pl.CostEstimate(flops=10**6, bytes_accessed=2 * 10**6, transcendentals=0),
        name="join",
    )(y, received, own, other, gates)


def around(value, x_core):
    return [value] + [move_ring(value, by, x_core) for by in (1, 3, 2)]


def local(
    residual,
    query_latent,
    query_rope,
    cache_latent,
    cache_rope,
    lengths,
    value_up,
    out_proj,
    gate_proj,
    up_proj,
    down_proj,
    groups,
    expert_picks,
    gate_levels,
):
    rows, model = residual.shape
    columns = out_proj.shape[1]
    dp = lax.axis_index("dp")
    z = lax.axis_index("tensor")
    core = dp % CORES
    chip = dp // CORES
    here_x, here_y = chip // SIDE, chip % SIDE

    quarter = model // PLANES
    sent = cut(down_proj[0])
    downs = [move_z(part, by) for part, by in zip(sent, (1, 3, 2))]

    kept, given, places_here = attend(
        query_latent, query_rope, cache_latent, cache_rope, lengths, value_up,
        (groups.T, expert_picks.T, gate_levels.T),
    )
    weighting = places_here == (jnp.arange(128) % CAP + 1).astype(bf16)
    weighting = weighting.astype(bf16)

    given = move_core(given)
    flat = jnp.where(
        core == 0, jnp.concatenate([kept, given], axis=0), jnp.concatenate([given, kept], axis=0)
    )
    blocks = jnp.concatenate(around(flat, 0), axis=0)

    spread = residual.reshape(rows, CHIPS * CORES, columns).transpose(1, 0, 2)
    spread, blocks, downs[:2] = lax.optimization_barrier((spread, blocks, downs[:2]))
    residual_columns = lax.all_to_all(spread, "dp", split_axis=0, concat_axis=0, tiled=True)
    residual_columns = residual_columns.reshape(CHIPS, CORES, rows, columns)

    blocks = around(blocks, 1)
    blocks[3], downs[2], residual_columns = lax.optimization_barrier(
        (blocks[3], downs[2], residual_columns)
    )
    swapped = [move_core(block) for block in blocks]
    low, high, places_all, levels_all = project(blocks, swapped, out_proj)
    low, high = sum_z(low, high)

    far = jnp.arange(SIDE, dtype=jnp.int32)
    x_far = (here_x - far) % SIDE
    y_far = (here_y - far) % SIDE
    x_spot = (x_far ^ (x_far >> 1))[:, None]
    y_spot = (y_far ^ (y_far >> 1))[None, :]
    table = jnp.where(core == 0, y_spot * SIDE + x_spot, x_spot * SIDE + y_spot)
    table = table.reshape(CHIPS).astype(jnp.int32)
    gates = gate_table(table, places_all, levels_all)
    outgoing = select(table, (low, high), residual_columns, places_all)
    outgoing, gates = lax.optimization_barrier((outgoing, gates))

    own = chip_exchange(outgoing)
    other = move_core(own)
    gate_weight = gate_proj.reshape(CHIPS, CORES, columns, -1)
    up_weight = up_proj.reshape(CHIPS, CORES, columns, -1)
    acc = up(own, gate_weight, up_weight)
    act = up(other, gate_weight, up_weight, acc)
    acts = [act] + [move_z(act, by) for by in (1, 3, 2)]
    made = down(acts, down_proj[0], downs, gates)
    pieces = made.reshape(CHIPS // QUARTER, CORES, PART, quarter)
    theirs = lax.dynamic_index_in_dim(pieces, 1 - core, 1, keepdims=False)
    received = move_core(theirs.reshape(CHIPS * CAP, quarter))
    returning = join(made, received, own, other, gates)
    returning = returning.reshape(CHIPS, CAP, quarter)
    returning, weighting = lax.optimization_barrier((returning, weighting))

    returned = chip_exchange(returning).reshape(CHIPS * CAP, quarter)
    mixed = jnp.dot(weighting, returned, preferred_element_type=f32).astype(bf16)
    turned = jnp.stack([mixed] + [move_z(mixed, by) for by in (1, 3, 2)])
    back = (z - jnp.arange(PLANES)) % PLANES
    spot = back ^ (back >> 1)
    return jnp.concatenate(
        [lax.dynamic_index_in_dim(turned, spot[k], 0, keepdims=False) for k in range(PLANES)], axis=1
    )


def solution(mesh):
    return jax.shard_map(
        local,
        mesh=mesh,
        in_specs=(
            P("dp", None),
            P("dp", "tensor", None),
            P("dp", "tensor", None),
            P("dp", None, None),
            P("dp", None, None),
            P("dp"),
            P("tensor", None, None),
            P("tensor", "dp"),
            P("dp", None, "tensor"),
            P("dp", None, "tensor"),
            P("dp", "tensor", None),
            P("dp", None),
            P("dp", None),
            P("dp", None),
        ),
        out_specs=P("dp", None),
        check_vma=False,
    )
```

```python
import jax
import jax.numpy as jnp
from jax import lax
from jax.experimental import pallas as pl
from jax.experimental.pallas import tpu as pltpu
from jax.sharding import PartitionSpec as P

SIDE = 4
CORES = 2
CHIPS = SIDE * SIDE
PLANES = 4
TOPG = 4
GROUPS = 8
EPG = 4
CAP = 8
QUARTER = 4
PART = QUARTER * CAP

score_scale = 192.0 ** (-0.5)
route_scale = 2.5
far_below = -1e30

f32 = jnp.float32
bf16 = jnp.bfloat16
VMEM = 28 * 1024 * 1024


def distant(value):
    return pltpu.with_memory_space_constraint(value, pltpu.HBM)


def dp_index(x, y, c):
    return (x * SIDE + y) * CORES + c


def place_pairs(place):
    return [
        (dp_index(x, y, c), dp_index(*place(x, y, c)))
        for x in range(SIDE)
        for y in range(SIDE)
        for c in range(CORES)
    ]


def move_core(value):
    return lax.ppermute(value, "dp", place_pairs(lambda x, y, c: (x, y, 1 - c)))


def move_ring(value, by, x_core):
    def place(x, y, c):
        return ((x + by) % SIDE, y, c) if c == x_core else (x, (y + by) % SIDE, c)

    return lax.ppermute(value, "dp", place_pairs(place))


def move_z(value, by):
    return lax.ppermute(value, "tensor", [(z, (z + by) % PLANES) for z in range(PLANES)])


def spread_z(value):
    copies = jnp.broadcast_to(value[None], (PLANES,) + value.shape)
    return lax.all_to_all(copies, "tensor", split_axis=0, concat_axis=0, tiled=True)


def sum_z(low, high):
    def add(block, mask):
        pairs = [(z, z ^ mask) for z in range(PLANES)]
        moved = lax.ppermute(block, "tensor", pairs)
        return (block.astype(f32) + moved.astype(f32)).astype(bf16)

    low, high = add(low, 1), add(high, 3)
    low, high = add(low, 3), add(high, 1)
    return low, high


def chip_exchange(value):
    groups = [[dp_index(x, y, c) for x in range(SIDE) for y in range(SIDE)] for c in range(CORES)]
    return lax.all_to_all(
        value, "dp", split_axis=0, concat_axis=0, axis_index_groups=groups, tiled=True
    )


DEPTH = 6


def this_core():
    return lax.axis_index("dp") % CORES


def quarter_lanes(by, width):
    z = lax.axis_index("tensor")
    return pl.ds(pl.multiple_of((z + by) % PLANES * width, width), width)


def upright(ref):
    rows = ref.shape[1]
    same = lax.broadcasted_iota(jnp.int32, (rows, rows), 0) == lax.broadcasted_iota(
        jnp.int32, (rows, rows), 1
    )
    turned = lax.dot_general(
        jnp.where(same, 1.0, 0.0).astype(bf16),
        ref[...].astype(f32).astype(bf16),
        (((1,), (1,)), ((), ())),
        preferred_element_type=f32,
    )
    return turned.astype(jnp.int32)


def route_tables(groups, picks, levels):
    rows = groups.shape[0]
    lane = lax.broadcasted_iota(jnp.int32, (rows, 128), 1)
    member = lane < 0
    for t in range(TOPG):
        member = member | (lane // 16 == groups[:, t : t + 1])
    below = lax.broadcasted_iota(jnp.int32, (rows, rows), 0) >= lax.broadcasted_iota(
        jnp.int32, (rows, rows), 1
    )
    counted = jnp.dot(
        jnp.where(below, 1.0, 0.0).astype(bf16),
        jnp.where(member, 1.0, 0.0).astype(bf16),
        preferred_element_type=f32,
    )
    places = jnp.where(member, counted, 0.0)
    table = jnp.where(lane - GROUPS * EPG == groups[:, :1], 1, 0)
    for k in range(picks.shape[1]):
        pick = picks[:, k : k + 1]
        group = jnp.zeros_like(pick)
        for t in range(TOPG):
            group = jnp.where(pick // EPG == t, groups[:, t : t + 1], group)
        table = jnp.where(lane == group * EPG + pick % EPG, levels[:, k : k + 1], table)
    return places.astype(bf16), table.astype(f32).astype(bf16)


def attend_kernel(
    lengths, q_ref, qr_ref, k_hbm, r_hbm, vu_hbm, dw_hbm, res_ref, groups_ref, picks_ref, levels_ref,
    kept_ref, given_ref, places_ref, spread_ref, cut_1, cut_3,
    k_ref, r_ref, mix_ref, vu_ref, cut_ref, sems, cut_sems, vu_sem,
):
    rows, heads, lat = q_ref.shape
    width = vu_ref.shape[2]
    cuts = (cut_1, cut_3)
    core = this_core()
    vu_copy = pltpu.make_async_copy(vu_hbm, vu_ref, vu_sem)

    def copies(row, slot):
        return (
            pltpu.make_async_copy(k_hbm.at[row], k_ref.at[slot], sems.at[0, slot]),
            pltpu.make_async_copy(r_hbm.at[row], r_ref.at[slot], sems.at[1, slot]),
        )

    entering, leaving = [], []
    for n, by in enumerate((1, 3)):
        lanes = quarter_lanes(by, cut_ref.shape[2])
        entering.append(pltpu.make_async_copy(dw_hbm.at[:, lanes], cut_ref.at[n], cut_sems.at[0, n]))
        leaving.append(pltpu.make_async_copy(cut_ref.at[n], cuts[n], cut_sems.at[1, n]))
    for row in range(DEPTH):
        for copy in copies(row, row):
            copy.start()
    for copy in entering:
        copy.start()
    vu_copy.start()

    columns = spread_ref.shape[2]
    for j in range(spread_ref.shape[0]):
        spread_ref[j] = res_ref[:, j * columns : (j + 1) * columns]
    places, levels = route_tables(upright(groups_ref), upright(picks_ref), upright(levels_ref))
    places_ref[...] = places
    half = heads * width // 2
    first = core == 0
    kept_ref[:, half:] = jnp.where(first, places.astype(f32), levels.astype(f32)).astype(bf16)
    given_ref[:, half:] = jnp.where(first, levels.astype(f32), places.astype(f32)).astype(bf16)

    def scores_of(row, slot):
        scores = lax.dot_general(
            q_ref[row], k_ref[slot], (((1,), (1,)), ((), ())), preferred_element_type=f32
        )
        return scores + jnp.dot(qr_ref[row], r_ref[slot], preferred_element_type=f32)

    def weights_of(scores, row):
        scores = scores * score_scale
        place = lax.broadcasted_iota(jnp.int32, scores.shape, 1)
        scores = jnp.where(place < lengths[row], scores, far_below)
        highest = jnp.max(scores, axis=1, keepdims=True)
        raised = jnp.exp(scores - highest)
        return (raised * (1.0 / jnp.sum(raised, axis=1, keepdims=True))).astype(bf16)

    def finish(scores, row, slot):
        mix = jnp.dot(weights_of(scores, row), k_ref[slot], preferred_element_type=f32)
        at = pl.ds(row * heads, heads)
        for j in range(mix_ref.shape[0]):
            mix_ref[j, at, :] = mix[:, j * 128 : (j + 1) * 128]

    def wait(row, slot):
        for copy in copies(row, slot):
            copy.wait()

    scored, weighed = {}, {}
    for row in range(rows + 2):
        if row < rows:
            wait(row, row % DEPTH)
            scored[row] = scores_of(row, row % DEPTH)
        if 0 <= row - 1 < rows:
            weighed[row - 1] = weights_of(scored.pop(row - 1), row - 1)
        if row >= 2:
            done = row - 2
            mix = jnp.dot(weighed.pop(done), k_ref[done % DEPTH], preferred_element_type=f32)
            at = pl.ds(done * heads, heads)
            for j in range(mix_ref.shape[0]):
                mix_ref[j, at, :] = mix[:, j * 128 : (j + 1) * 128]
            if done + DEPTH < rows:
                for copy in copies(done + DEPTH, done % DEPTH):
                    copy.start()
        if row == DEPTH:
            for n, copy in enumerate(entering):
                copy.wait()
                leaving[n].start()
    vu_copy.wait()
    for side, ref in ((core, kept_ref), (1 - core, given_ref)):
        for i in range(heads // 2):
            h = side * (heads // 2) + i
            left = [mix_ref[j, pl.ds(h, rows, stride=heads), :] for j in range(mix_ref.shape[0])]
            left = jnp.concatenate(left, axis=1).astype(bf16)
            ref[:, i * width : (i + 1) * width] = jnp.dot(
                left, vu_ref[h], preferred_element_type=f32
            ).astype(bf16)
    for copy in leaving:
        copy.wait()


def attend(
    query_latent, query_rope, cache_latent, cache_rope, lengths, value_up, down_weight, residual, columns, routing
):
    rows, heads, lat = query_latent.shape
    rope = query_rope.shape[2]
    positions = cache_latent.shape[1]
    width = value_up.shape[2]
    units, model = down_weight.shape
    whole = pl.BlockSpec(memory_space=pltpu.VMEM)
    small = pl.BlockSpec(memory_space=pltpu.SMEM)
    far = pl.BlockSpec(memory_space=pltpu.HBM)
    return pl.pallas_call(
        attend_kernel,
        in_specs=[small, whole, whole] + [far] * 4 + [whole] * 4,
        out_specs=(whole,) * 4 + (far,) * 2,
        out_shape=(
            jax.ShapeDtypeStruct((rows, heads * width // 2 + 128), bf16),
            jax.ShapeDtypeStruct((rows, heads * width // 2 + 128), bf16),
            jax.ShapeDtypeStruct((rows, 128), bf16),
            jax.ShapeDtypeStruct((residual.shape[1] // columns, rows, columns), bf16),
        )
        + (jax.ShapeDtypeStruct((units, model // PLANES), bf16),) * 2,
        scratch_shapes=[
            pltpu.VMEM((DEPTH, positions, lat), bf16),
            pltpu.VMEM((DEPTH, rope, positions), bf16),
            pltpu.VMEM((lat // 128, rows * heads, 128), f32),
            pltpu.VMEM((heads, lat, width), bf16),
            pltpu.VMEM((2, units, model // PLANES), bf16),
            pltpu.SemaphoreType.DMA((2, DEPTH)),
            pltpu.SemaphoreType.DMA((2, 2)),
            pltpu.SemaphoreType.DMA,
        ],
        compiler_params=pltpu.CompilerParams(vmem_limit_bytes=VMEM),
        cost_estimate=pl.CostEstimate(
            flops=4 * rows * heads * positions * lat,
            bytes_accessed=2 * rows * positions * (lat + rope),
            transcendentals=rows * heads * positions,
        ),
        name="attend",
    )(
        lengths, query_latent, query_rope, distant(cache_latent), distant(cache_rope), distant(value_up),
        distant(down_weight), residual, *routing,
    )


def half_product(blocks, w_hbm, w_ref, sem, side):
    half = w_ref.shape[1]
    copy = pltpu.make_async_copy(
        w_hbm.at[:, pl.ds(pl.multiple_of(side * half, half), half)], w_ref, sem
    )
    copy.start()
    left = jnp.concatenate([block[:, :half] for block in blocks])
    copy.wait()
    terms = lax.dot_general(left, w_ref[...], (((1,), (1,)), ((), ())), preferred_element_type=f32)
    span = terms.shape[0] // SIDE
    return [terms[i * span : (i + 1) * span] for i in range(SIDE)]


def first_half_kernel(*refs):
    blocks, w_hbm, out_ref, table_ref, w_ref, sem = refs[:SIDE], *refs[SIDE:]
    for i, terms in enumerate(half_product(blocks, w_hbm, w_ref, sem, this_core())):
        out_ref[i] = terms
        table_ref[i] = blocks[i][:, w_ref.shape[1] :]


def second_half_kernel(*refs):
    blocks, w_hbm, made_ref, own_ref = refs[:SIDE], *refs[SIDE : SIDE + 3]
    low_ref, high_ref, places_ref, levels_ref, w_ref, sem = refs[SIDE + 3 :]
    core = this_core()
    half = w_ref.shape[1]
    made = half_product(blocks, w_hbm, w_ref, sem, 1 - core)
    rows = made[0].shape[0] // SIDE
    first = core == 0
    for i in range(SIDE):
        for j in range(SIDE):
            at, across = slice(j * rows, (j + 1) * rows), slice(i * rows, (i + 1) * rows)
            total = (made_ref[i, at] + made[j][across]).astype(bf16)
            (low_ref if i < 2 else high_ref)[i % 2 * SIDE + j] = total
            mine = own_ref[i, at].astype(f32)
            theirs = blocks[j][across, half:].astype(f32)
            places_ref[i * SIDE + j] = jnp.where(first, mine, theirs).astype(bf16)
            levels_ref[i * SIDE + j] = jnp.where(first, theirs, mine).astype(bf16)


def project(blocks, out_proj, before=None):
    columns = out_proj.shape[1]
    tall = blocks[0].shape[0]
    rows = tall // SIDE
    whole = pl.BlockSpec(memory_space=pltpu.VMEM)
    far = pl.BlockSpec(memory_space=pltpu.HBM)
    if before is None:
        out_shape = (
            jax.ShapeDtypeStruct((SIDE, tall, columns), f32),
            jax.ShapeDtypeStruct((SIDE, tall, 128), bf16),
        )
    else:
        sums = jax.ShapeDtypeStruct((CHIPS // 2, rows, columns), bf16)
        table = pltpu.HBM((CHIPS, rows, 128), bf16)
        out_shape = (sums, sums, table, table)
    before = before or ()
    return pl.pallas_call(
        second_half_kernel if before else first_half_kernel,
        in_specs=[whole] * SIDE + [far] + [whole] * len(before),
        out_specs=(whole,) * len(out_shape),
        out_shape=out_shape,
        scratch_shapes=[
            pltpu.VMEM((columns, out_proj.shape[0] // 2), bf16),
            pltpu.SemaphoreType.DMA,
        ],
        compiler_params=pltpu.CompilerParams(vmem_limit_bytes=VMEM),
        cost_estimate=pl.CostEstimate(flops=5 * 10**8, bytes_accessed=4 * 10**6, transcendentals=0),
        name="project",
    )(*blocks, distant(out_proj.T), *before)


def slot_masks(mark, rows):
    lane = lax.broadcasted_iota(jnp.int32, (2 * rows, 128), 1)
    wanted = (lane % CAP + 1).astype(f32)
    second = lax.broadcasted_iota(jnp.int32, (2 * rows, 128), 0) >= rows
    right_half = (lane % (2 * CAP) >= CAP) == second
    return jnp.where((mark == wanted) & right_half, 1.0, 0.0).astype(bf16)


def gate_kernel(table, places_ref, levels_ref, out_ref, made_ref):
    dp = lax.axis_index("dp")
    group = dp // EPG
    rows = places_ref.shape[1] // CORES
    lane = lax.broadcasted_iota(jnp.int32, (2 * rows, 128), 1)
    for quarter in range(CHIPS // QUARTER):
        for parity in range(CORES):
            for pair in range(QUARTER // 2):
                chips = (quarter * QUARTER + 2 * pair, quarter * QUARTER + 2 * pair + 1)
                at = slice(parity * rows, (parity + 1) * rows)
                mark = jnp.concatenate([places_ref[table[chip], at].astype(f32) for chip in chips])
                level = jnp.concatenate([levels_ref[table[chip], at].astype(f32) for chip in chips])
                total = jnp.sum(jnp.where(lane < GROUPS * EPG, level, 0.0), axis=1, keepdims=True)
                mine = jnp.sum(jnp.where(lane == dp, level, 0.0), axis=1, keepdims=True)
                home = jnp.sum(
                    jnp.where(lane == GROUPS * EPG + group, level, 0.0), axis=1, keepdims=True
                )
                gate = route_scale * mine / total
                high = gate.astype(bf16).astype(f32)
                values = jnp.where(lane == 0, high, jnp.where(lane == 1, gate - high, 0.0))
                values = jnp.where(lane == 2, home, values).astype(bf16)
                made_ref[...] = lax.dot_general(
                    slot_masks(mark, rows), values, (((0,), (0,)), ((), ())),
                    preferred_element_type=f32,
                )
                to = quarter * CORES * PART + parity * PART + pair * 2 * CAP
                out_ref[to : to + 2 * CAP] = made_ref[
                    pl.ds(pl.multiple_of(group * 2 * CAP, 2 * CAP), 2 * CAP)
                ]


def gate_table(table, places, levels):
    whole = pl.BlockSpec(memory_space=pltpu.VMEM)
    return pl.pallas_call(
        gate_kernel,
        in_specs=[pl.BlockSpec(memory_space=pltpu.SMEM), whole, whole],
        out_specs=whole,
        out_shape=jax.ShapeDtypeStruct((CHIPS * CORES * CAP, 128), f32),
        scratch_shapes=[pltpu.VMEM((128, 128), f32)],
        compiler_params=pltpu.CompilerParams(vmem_limit_bytes=VMEM),
        cost_estimate=pl.CostEstimate(flops=10**8, bytes_accessed=10**6, transcendentals=0),
        name="gate_table",
    )(table, distant(places), distant(levels))


def select_kernel(table, low_ref, high_ref, res_ref, places_ref, out_ref):
    rows = res_ref.shape[2]

    def attention_of(parity, chip):
        place = table[chip]
        side = CHIPS // 2
        inside = place % side
        at = slice(parity * rows, (parity + 1) * rows)
        return jnp.where(place < side, low_ref[inside, at].astype(f32), high_ref[inside, at].astype(f32))

    for parity in range(CORES):
        for pair in range(QUARTER // 2):
            quarters = []
            for quarter in range(CHIPS // QUARTER):
                parts = []
                marks = []
                for chip in (quarter * QUARTER + 2 * pair, quarter * QUARTER + 2 * pair + 1):
                    attention = attention_of(parity, chip)
                    parts.append((res_ref[chip, parity].astype(f32) + attention).astype(bf16))
                    at = slice(parity * rows, (parity + 1) * rows)
                    marks.append(places_ref[table[chip], at].astype(f32))
                hidden = jnp.concatenate(parts, axis=0)
                mark = jnp.concatenate(marks, axis=0)
                pick = slot_masks(mark, rows)
                quarters.append(
                    lax.dot_general(
                        pick, hidden, (((0,), (0,)), ((), ())), preferred_element_type=f32
                    )
                )
            chosen = jnp.concatenate(quarters, axis=1).astype(bf16)
            at = parity * PART + pair * 2 * CAP
            for group in range(GROUPS):
                block = chosen[group * 2 * CAP : (group + 1) * 2 * CAP]
                out_ref[2 * group, at : at + 2 * CAP, :] = block
                out_ref[2 * group + 1, at : at + 2 * CAP, :] = block


def select(table, parts, residual, places):
    columns = residual.shape[-1]
    whole = pl.BlockSpec(memory_space=pltpu.VMEM)
    return pl.pallas_call(
        select_kernel,
        in_specs=[pl.BlockSpec(memory_space=pltpu.SMEM)] + [whole] * 4,
        out_specs=whole,
        out_shape=jax.ShapeDtypeStruct(
            (CHIPS, CORES * PART, CHIPS // QUARTER * columns), bf16
        ),
        compiler_params=pltpu.CompilerParams(vmem_limit_bytes=VMEM),
        cost_estimate=pl.CostEstimate(flops=10**9, bytes_accessed=6 * 10**6, transcendentals=0),
        name="select",
    )(table, *parts, distant(residual), distant(places))


def unpacked(block, columns):
    parts = [block[:, q * columns : (q + 1) * columns] for q in range(CHIPS // QUARTER)]
    return jnp.concatenate(parts, axis=0)


def raise_up(x_ref, gw_hbm, uw_hbm, w_ref, sems, core, acc):
    columns, units = gw_hbm.shape[2:]
    span = CHIPS // QUARTER
    copies = []
    for part in range(QUARTER):
        chips = pl.ds(part * span, span)
        for n, source in enumerate((gw_hbm, uw_hbm)):
            lanes = slice(n * units, (n + 1) * units)
            copies.append(
                pltpu.make_async_copy(
                    source.at[chips, core], w_ref.at[chips, :, lanes], sems.at[part, n]
                )
            )
    for copy in copies:
        copy.start()
    for chip in range(CHIPS):
        if chip % span == 0:
            copies[chip // span * 2].wait()
            copies[chip // span * 2 + 1].wait()
        acc = acc + jnp.dot(unpacked(x_ref[chip], columns), w_ref[chip], preferred_element_type=f32)
    return acc


def up_kernel(x_ref, gw_hbm, uw_hbm, acc_ref, w_ref, sems):
    zero = jnp.zeros(acc_ref.shape, f32)
    acc_ref[...] = raise_up(x_ref, gw_hbm, uw_hbm, w_ref, sems, this_core(), zero)


def act_kernel(acc_ref, x_ref, gw_hbm, uw_hbm, act_ref, w_ref, sems):
    acc = raise_up(x_ref, gw_hbm, uw_hbm, w_ref, sems, 1 - this_core(), acc_ref[...])
    units = acc.shape[1] // 2
    gated = acc[:, :units]
    act_ref[...] = (gated / (1.0 + jnp.exp(-gated)) * acc[:, units:]).astype(bf16)


def up(x, gate_weight, up_weight, before=None):
    columns, units = gate_weight.shape[2:]
    slots = x.shape[1] * CHIPS // QUARTER
    whole = pl.BlockSpec(memory_space=pltpu.VMEM)
    far = pl.BlockSpec(memory_space=pltpu.HBM)
    operands = (x,) if before is None else (before, x)
    return pl.pallas_call(
        up_kernel if before is None else act_kernel,
        in_specs=[whole] * len(operands) + [far, far],
        out_specs=whole,
        out_shape=(
            jax.ShapeDtypeStruct((slots, 2 * units), f32)
            if before is None
            else jax.ShapeDtypeStruct((slots, units), bf16)
        ),
        scratch_shapes=[
            pltpu.VMEM((CHIPS, columns, 2 * units), bf16),
            pltpu.SemaphoreType.DMA((QUARTER, 2)),
        ],
        compiler_params=pltpu.CompilerParams(vmem_limit_bytes=VMEM),
        cost_estimate=pl.CostEstimate(
            flops=4 * CHIPS * slots * columns * units, bytes_accessed=6 * 10**6, transcendentals=0
        ),
        name="up",
    )(*operands, distant(gate_weight), distant(up_weight))


def cut_kernel(w_hbm, out_ref):
    pltpu.sync_copy(w_hbm.at[:, quarter_lanes(2, out_ref.shape[1])], out_ref)


def cut(down_weight):
    units, width = down_weight.shape
    return pl.pallas_call(
        cut_kernel,
        in_specs=[pl.BlockSpec(memory_space=pltpu.HBM)],
        out_specs=pl.BlockSpec(memory_space=pltpu.VMEM),
        out_shape=jax.ShapeDtypeStruct((units, width // PLANES), bf16),
        compiler_params=pltpu.CompilerParams(vmem_limit_bytes=VMEM),
        cost_estimate=pl.CostEstimate(flops=0, bytes_accessed=2 * 10**6, transcendentals=0),
        name="cut",
    )(distant(down_weight))


def down_kernel(a0, a1, a2, a3, own_hbm, w1, w2, w3, gates_ref, out_ref, w_ref, sems):
    acts = (a0, a1, a2, a3)
    z = lax.axis_index("tensor")
    units = a0.shape[1]
    width = out_ref.shape[1]
    lanes = pl.ds(pl.multiple_of(z * width, width), width)
    copies = [
        pltpu.make_async_copy(source, w_ref.at[n * units : (n + 1) * units], sems.at[n])
        for n, source in enumerate((own_hbm.at[:, lanes], w1, w2, w3))
    ]
    for copy in copies:
        copy.start()
    gate = gates_ref[:, 0:1] + gates_ref[:, 1:2]
    left = jnp.concatenate([act[...] for act in acts], axis=1)
    for copy in copies:
        copy.wait()
    block = 256
    for at in range(0, width, block):
        made = jnp.dot(left, w_ref[:, at : at + block], preferred_element_type=f32)
        out_ref[:, at : at + block] = (made * gate).astype(bf16)


def down(acts, own_weight, weights, gates):
    slots = acts[0].shape[0]
    units, width = weights[0].shape
    whole = pl.BlockSpec(memory_space=pltpu.VMEM)
    far = pl.BlockSpec(memory_space=pltpu.HBM)
    return pl.pallas_call(
        down_kernel,
        in_specs=[whole] * 4 + [far] * 4 + [whole],
        out_specs=whole,
        out_shape=jax.ShapeDtypeStruct((slots, width), bf16),
        scratch_shapes=[
            pltpu.VMEM((PLANES * units, width), bf16),
            pltpu.SemaphoreType.DMA((PLANES,)),
        ],
        compiler_params=pltpu.CompilerParams(vmem_limit_bytes=VMEM),
        cost_estimate=pl.CostEstimate(
            flops=8 * slots * units * width, bytes_accessed=6 * 10**6, transcendentals=0
        ),
        name="down",
    )(*acts, distant(own_weight), *[distant(weight) for weight in weights], gates)


def join_kernel(y_ref, received_ref, own_hbm, other_hbm, gates_ref, out_ref, x_ref, sems):
    half, width = out_ref.shape
    columns = own_hbm.shape[2] // (CHIPS // QUARTER)
    dp, z = lax.axis_index("dp"), lax.axis_index("tensor")
    core = dp % CORES
    step_here = dp // CORES % 2
    chips = QUARTER // 2
    near = pl.ds(z * QUARTER + step_here * chips, chips)
    rows = pl.ds(pl.multiple_of(core * PART, PART), PART)
    copies = [
        pltpu.make_async_copy(source.at[near, rows], x_ref.at[n], sems.at[n])
        for n, source in enumerate((own_hbm, other_hbm))
    ]
    for copy in copies:
        copy.start()
    both, homes = [], []
    for q in range(CHIPS // QUARTER):
        at = pl.ds(pl.multiple_of(q * CORES * PART + core * PART, PART), PART)
        both.append(y_ref[at, :].astype(f32) + received_ref[q * PART : (q + 1) * PART, :].astype(f32))
        homes.append(gates_ref[at, 2:3])
    total = jnp.concatenate(both, axis=0)
    home = jnp.concatenate(homes, axis=0)
    out_ref[...] = total.astype(bf16)
    for copy in copies:
        copy.wait()
    block = chips * CORES * columns
    flip = core == 1
    parts = []
    for chip in range(chips):
        mine = unpacked(x_ref[0, chip].astype(f32), columns)
        theirs = unpacked(x_ref[1, chip].astype(f32), columns)
        parts.append(jnp.where(flip, theirs, mine))
        parts.append(jnp.where(flip, mine, theirs))
    hidden = jnp.concatenate(parts, axis=1) * home
    for step in range(width // block):

        @pl.when(step_here == step)
        def _():
            at = slice(step * block, (step + 1) * block)
            out_ref[:, at] = (total[:, at] + hidden).astype(bf16)


def join(y, received, own, other, gates):
    whole = pl.BlockSpec(memory_space=pltpu.VMEM)
    far = pl.BlockSpec(memory_space=pltpu.HBM)
    return pl.pallas_call(
        join_kernel,
        in_specs=[whole, whole, far, far, whole],
        out_specs=whole,
        out_shape=jax.ShapeDtypeStruct(received.shape, bf16),
        scratch_shapes=[
            pltpu.VMEM((2, QUARTER // 2, PART, own.shape[2]), bf16),
            pltpu.SemaphoreType.DMA((2,)),
        ],
        compiler_params=pltpu.CompilerParams(vmem_limit_bytes=VMEM),
        cost_estimate=pl.CostEstimate(flops=10**6, bytes_accessed=2 * 10**6, transcendentals=0),
        name="join",
    )(y, received, own, other, gates)


def around(value, x_core):
    return [value] + [move_ring(value, by, x_core) for by in (1, 3, 2)]


def local(
    residual,
    query_latent,
    query_rope,
    cache_latent,
    cache_rope,
    lengths,
    value_up,
    out_proj,
    gate_proj,
    up_proj,
    down_proj,
    groups,
    expert_picks,
    gate_levels,
):
    rows, model = residual.shape
    columns = out_proj.shape[1]
    dp = lax.axis_index("dp")
    z = lax.axis_index("tensor")
    core = dp % CORES
    chip = dp // CORES
    here_x, here_y = chip // SIDE, chip % SIDE

    quarter = model // PLANES
    opposite = move_z(cut(down_proj[0]), 2)

    kept, given, places_here, spread, *sent = attend(
        query_latent, query_rope, cache_latent, cache_rope, lengths, value_up, down_proj[0], residual, columns,
        (groups.T, expert_picks.T, gate_levels.T),
    )
    weighting = places_here == (jnp.arange(128) % CAP + 1).astype(bf16)
    weighting = weighting.astype(bf16)

    given = move_core(given)
    flat = jnp.where(
        core == 0, jnp.concatenate([kept, given], axis=0), jnp.concatenate([given, kept], axis=0)
    )
    blocks = jnp.concatenate(around(flat, 0), axis=0)

    spread, blocks, opposite = lax.optimization_barrier((spread, blocks, opposite))
    residual_columns = lax.all_to_all(spread, "dp", split_axis=0, concat_axis=0, tiled=True)
    downs = [move_z(part, by) for part, by in zip(sent, (1, 3))] + [opposite]
    residual_columns = residual_columns.reshape(CHIPS, CORES, rows, columns)

    blocks = around(blocks, 1)
    blocks[3], downs[:2], residual_columns = lax.optimization_barrier(
        (blocks[3], downs[:2], residual_columns)
    )
    swapped = [move_core(block) for block in blocks]
    low, high, places_all, levels_all = project(swapped, out_proj, project(blocks, out_proj))
    low, high = sum_z(low, high)

    far = jnp.arange(SIDE, dtype=jnp.int32)
    x_far = (here_x - far) % SIDE
    y_far = (here_y - far) % SIDE
    x_spot = (x_far ^ (x_far >> 1))[:, None]
    y_spot = (y_far ^ (y_far >> 1))[None, :]
    table = jnp.where(core == 0, y_spot * SIDE + x_spot, x_spot * SIDE + y_spot)
    table = table.reshape(CHIPS).astype(jnp.int32)
    gates = gate_table(table, places_all, levels_all)
    outgoing = select(table, (low, high), residual_columns, places_all)
    outgoing, gates = lax.optimization_barrier((outgoing, gates))

    own = chip_exchange(outgoing)
    other = move_core(own)
    gate_weight = gate_proj.reshape(CHIPS, CORES, columns, -1)
    up_weight = up_proj.reshape(CHIPS, CORES, columns, -1)
    acc = up(own, gate_weight, up_weight)
    act = up(other, gate_weight, up_weight, acc)
    acts = [act] + [move_z(act, by) for by in (1, 3, 2)]
    made = down(acts, down_proj[0], downs, gates)
    pieces = made.reshape(CHIPS // QUARTER, CORES, PART, quarter)
    theirs = lax.dynamic_index_in_dim(pieces, 1 - core, 1, keepdims=False)
    received = move_core(theirs.reshape(CHIPS * CAP, quarter))
    returning = join(made, received, own, other, gates)
    returning = returning.reshape(CHIPS, CAP, quarter)
    returning, weighting = lax.optimization_barrier((returning, weighting))

    returned = chip_exchange(returning).reshape(CHIPS * CAP, quarter)
    mixed = jnp.dot(weighting, returned, preferred_element_type=f32).astype(bf16)
    return spread_z(mixed).transpose(1, 0, 2).reshape(rows, model)


def solution(mesh):
    return jax.shard_map(
        local,
        mesh=mesh,
        in_specs=(
            P("dp", None),
            P("dp", "tensor", None),
            P("dp", "tensor", None),
            P("dp", None, None),
            P("dp", None, None),
            P("dp"),
            P("tensor", None, None),
            P("tensor", "dp"),
            P("dp", None, "tensor"),
            P("dp", None, "tensor"),
            P("dp", "tensor", None),
            P("dp", None),
            P("dp", None),
            P("dp", None),
        ),
        out_specs=P("dp", None),
        check_vma=False,
    )
```

```python
import jax
import jax.numpy as jnp
from jax import lax
from jax.experimental import pallas as pl
from jax.experimental.pallas import tpu as pltpu
from jax.sharding import PartitionSpec as P

SIDE = 4
CORES = 2
CHIPS = SIDE * SIDE
PLANES = 4
TOPG = 4
GROUPS = 8
EPG = 4
CAP = 8
QUARTER = 4
PART = QUARTER * CAP

score_scale = 192.0 ** (-0.5)
route_scale = 2.5
far_below = -1e30

f32 = jnp.float32
bf16 = jnp.bfloat16
VMEM = 28 * 1024 * 1024


def distant(value):
    return pltpu.with_memory_space_constraint(value, pltpu.HBM)


def dp_index(x, y, c):
    return (x * SIDE + y) * CORES + c


def place_pairs(place):
    return [
        (dp_index(x, y, c), dp_index(*place(x, y, c)))
        for x in range(SIDE)
        for y in range(SIDE)
        for c in range(CORES)
    ]


def move_core(value):
    return lax.ppermute(value, "dp", place_pairs(lambda x, y, c: (x, y, 1 - c)))


def move_ring(value, by, x_core):
    def place(x, y, c):
        return ((x + by) % SIDE, y, c) if c == x_core else (x, (y + by) % SIDE, c)

    return lax.ppermute(value, "dp", place_pairs(place))


def move_z(value, by):
    return lax.ppermute(value, "tensor", [(z, (z + by) % PLANES) for z in range(PLANES)])


def spread_z(value):
    copies = jnp.broadcast_to(value[None], (PLANES,) + value.shape)
    return lax.all_to_all(copies, "tensor", split_axis=0, concat_axis=0, tiled=True)


def sum_z(low, high):
    def add(block, mask):
        pairs = [(z, z ^ mask) for z in range(PLANES)]
        moved = lax.ppermute(block, "tensor", pairs)
        return (block.astype(f32) + moved.astype(f32)).astype(bf16)

    low, high = add(low, 1), add(high, 3)
    low, high = add(low, 3), add(high, 1)
    return low, high


def chip_exchange(value):
    groups = [[dp_index(x, y, c) for x in range(SIDE) for y in range(SIDE)] for c in range(CORES)]
    return lax.all_to_all(
        value, "dp", split_axis=0, concat_axis=0, axis_index_groups=groups, tiled=True
    )


DEPTH = 6


def this_core():
    return lax.axis_index("dp") % CORES


def quarter_lanes(by, width):
    z = lax.axis_index("tensor")
    return pl.ds(pl.multiple_of((z + by) % PLANES * width, width), width)


def upright(ref):
    rows = ref.shape[1]
    same = lax.broadcasted_iota(jnp.int32, (rows, rows), 0) == lax.broadcasted_iota(
        jnp.int32, (rows, rows), 1
    )
    turned = lax.dot_general(
        jnp.where(same, 1.0, 0.0).astype(bf16),
        ref[...].astype(f32).astype(bf16),
        (((1,), (1,)), ((), ())),
        preferred_element_type=f32,
    )
    return turned.astype(jnp.int32)


def route_tables(groups, picks, levels):
    rows = groups.shape[0]
    lane = lax.broadcasted_iota(jnp.int32, (rows, 128), 1)
    member = lane < 0
    for t in range(TOPG):
        member = member | (lane // 16 == groups[:, t : t + 1])
    below = lax.broadcasted_iota(jnp.int32, (rows, rows), 0) >= lax.broadcasted_iota(
        jnp.int32, (rows, rows), 1
    )
    counted = jnp.dot(
        jnp.where(below, 1.0, 0.0).astype(bf16),
        jnp.where(member, 1.0, 0.0).astype(bf16),
        preferred_element_type=f32,
    )
    places = jnp.where(member, counted, 0.0)
    table = jnp.where(lane - GROUPS * EPG == groups[:, :1], 1, 0)
    for k in range(picks.shape[1]):
        pick = picks[:, k : k + 1]
        group = jnp.zeros_like(pick)
        for t in range(TOPG):
            group = jnp.where(pick // EPG == t, groups[:, t : t + 1], group)
        table = jnp.where(lane == group * EPG + pick % EPG, levels[:, k : k + 1], table)
    return places.astype(bf16), table.astype(f32).astype(bf16)


def attend_kernel(
    lengths, q_ref, qr_ref, k_hbm, r_hbm, vu_hbm, dw_hbm, res_ref, groups_ref, picks_ref, levels_ref,
    out_ref, places_ref, spread_ref, cut_1, cut_3,
    k_ref, r_ref, mix_ref, vu_ref, cut_ref, sems, cut_sems, vu_sem,
):
    rows, heads, lat = q_ref.shape
    width = vu_ref.shape[2]
    cuts = (cut_1, cut_3)
    vu_copy = pltpu.make_async_copy(vu_hbm, vu_ref, vu_sem)

    def copies(row, slot):
        return (
            pltpu.make_async_copy(k_hbm.at[row], k_ref.at[slot], sems.at[0, slot]),
            pltpu.make_async_copy(r_hbm.at[row], r_ref.at[slot], sems.at[1, slot]),
        )

    entering, leaving = [], []
    for n, by in enumerate((1, 3)):
        lanes = quarter_lanes(by, cut_ref.shape[2])
        entering.append(pltpu.make_async_copy(dw_hbm.at[:, lanes], cut_ref.at[n], cut_sems.at[0, n]))
        leaving.append(pltpu.make_async_copy(cut_ref.at[n], cuts[n], cut_sems.at[1, n]))
    for row in range(DEPTH):
        for copy in copies(row, row):
            copy.start()
    for copy in entering:
        copy.start()
    vu_copy.start()

    columns = spread_ref.shape[2]
    for j in range(spread_ref.shape[0]):
        spread_ref[j] = res_ref[:, j * columns : (j + 1) * columns]
    places, levels = route_tables(upright(groups_ref), upright(picks_ref), upright(levels_ref))
    places_ref[...] = places
    out_ref[:, heads * width : heads * width + 128] = places
    out_ref[:, heads * width + 128 :] = levels

    def scores_of(row, slot):
        scores = lax.dot_general(
            q_ref[row], k_ref[slot], (((1,), (1,)), ((), ())), preferred_element_type=f32
        )
        return scores + jnp.dot(qr_ref[row], r_ref[slot], preferred_element_type=f32)

    def weights_of(scores, row):
        scores = scores * score_scale
        place = lax.broadcasted_iota(jnp.int32, scores.shape, 1)
        scores = jnp.where(place < lengths[row], scores, far_below)
        highest = jnp.max(scores, axis=1, keepdims=True)
        raised = jnp.exp(scores - highest)
        return (raised * (1.0 / jnp.sum(raised, axis=1, keepdims=True))).astype(bf16)

    def finish(scores, row, slot):
        mix = jnp.dot(weights_of(scores, row), k_ref[slot], preferred_element_type=f32)
        at = pl.ds(row * heads, heads)
        for j in range(mix_ref.shape[0]):
            mix_ref[j, at, :] = mix[:, j * 128 : (j + 1) * 128]

    def wait(row, slot):
        for copy in copies(row, slot):
            copy.wait()

    scored, weighed = {}, {}
    for row in range(rows + 2):
        if row < rows:
            wait(row, row % DEPTH)
            scored[row] = scores_of(row, row % DEPTH)
        if 0 <= row - 1 < rows:
            weighed[row - 1] = weights_of(scored.pop(row - 1), row - 1)
        if row >= 2:
            done = row - 2
            mix = jnp.dot(weighed.pop(done), k_ref[done % DEPTH], preferred_element_type=f32)
            at = pl.ds(done * heads, heads)
            for j in range(mix_ref.shape[0]):
                mix_ref[j, at, :] = mix[:, j * 128 : (j + 1) * 128]
            if done + DEPTH < rows:
                for copy in copies(done + DEPTH, done % DEPTH):
                    copy.start()
        if row == DEPTH:
            for n, copy in enumerate(entering):
                copy.wait()
                leaving[n].start()
    vu_copy.wait()
    for h in range(heads):
        left = [mix_ref[j, pl.ds(h, rows, stride=heads), :] for j in range(mix_ref.shape[0])]
        left = jnp.concatenate(left, axis=1).astype(bf16)
        out_ref[:, h * width : (h + 1) * width] = jnp.dot(
            left, vu_ref[h], preferred_element_type=f32
        ).astype(bf16)
    for copy in leaving:
        copy.wait()


def attend(
    query_latent, query_rope, cache_latent, cache_rope, lengths, value_up, down_weight, residual, columns, routing
):
    rows, heads, lat = query_latent.shape
    rope = query_rope.shape[2]
    positions = cache_latent.shape[1]
    width = value_up.shape[2]
    units, model = down_weight.shape
    whole = pl.BlockSpec(memory_space=pltpu.VMEM)
    small = pl.BlockSpec(memory_space=pltpu.SMEM)
    far = pl.BlockSpec(memory_space=pltpu.HBM)
    return pl.pallas_call(
        attend_kernel,
        in_specs=[small, whole, whole] + [far] * 4 + [whole] * 4,
        out_specs=(whole,) * 3 + (far,) * 2,
        out_shape=(
            jax.ShapeDtypeStruct((rows, heads * width + 2 * 128), bf16),
            jax.ShapeDtypeStruct((rows, 128), bf16),
            jax.ShapeDtypeStruct((residual.shape[1] // columns, rows, columns), bf16),
        )
        + (jax.ShapeDtypeStruct((units, model // PLANES), bf16),) * 2,
        scratch_shapes=[
            pltpu.VMEM((DEPTH, positions, lat), bf16),
            pltpu.VMEM((DEPTH, rope, positions), bf16),
            pltpu.VMEM((lat // 128, rows * heads, 128), f32),
            pltpu.VMEM((heads, lat, width), bf16),
            pltpu.VMEM((2, units, model // PLANES), bf16),
            pltpu.SemaphoreType.DMA((2, DEPTH)),
            pltpu.SemaphoreType.DMA((2, 2)),
            pltpu.SemaphoreType.DMA,
        ],
        compiler_params=pltpu.CompilerParams(vmem_limit_bytes=VMEM),
        cost_estimate=pl.CostEstimate(
            flops=4 * rows * heads * positions * lat,
            bytes_accessed=2 * rows * positions * (lat + rope),
            transcendentals=rows * heads * positions,
        ),
        name="attend",
    )(
        lengths, query_latent, query_rope, distant(cache_latent), distant(cache_rope), distant(value_up),
        distant(down_weight), residual, *routing,
    )


def project_kernel(*refs):
    blocks, w_hbm = refs[:SIDE], refs[SIDE]
    out_ref, places_ref, levels_ref, w_ref, sem = refs[SIDE + 1 :]
    depth = w_ref.shape[1]
    copy = pltpu.make_async_copy(w_hbm, w_ref, sem)
    copy.start()
    left = jnp.concatenate([block[:, :depth] for block in blocks])
    rows = out_ref.shape[1]
    for i, block in enumerate(blocks):
        for j in range(SIDE):
            at = slice(j * rows, (j + 1) * rows)
            places_ref[i * SIDE + j] = block[at, depth : depth + 128]
            levels_ref[i * SIDE + j] = block[at, depth + 128 :]
    copy.wait()
    made = lax.dot_general(left, w_ref[...], (((1,), (1,)), ((), ())), preferred_element_type=f32)
    made = made.astype(bf16)
    for n in range(CHIPS):
        out_ref[n] = made[n * rows : (n + 1) * rows]


def project(blocks, out_proj):
    depth, columns = out_proj.shape
    rows = blocks[0].shape[0] // SIDE
    whole = pl.BlockSpec(memory_space=pltpu.VMEM)
    far = pl.BlockSpec(memory_space=pltpu.HBM)
    table = pltpu.HBM((CHIPS, rows, 128), bf16)
    return pl.pallas_call(
        project_kernel,
        in_specs=[whole] * SIDE + [far],
        out_specs=(whole,) * 3,
        out_shape=(jax.ShapeDtypeStruct((CHIPS, rows, columns), bf16), table, table),
        scratch_shapes=[pltpu.VMEM((columns, depth), bf16), pltpu.SemaphoreType.DMA],
        compiler_params=pltpu.CompilerParams(vmem_limit_bytes=VMEM),
        cost_estimate=pl.CostEstimate(flops=5 * 10**8, bytes_accessed=4 * 10**6, transcendentals=0),
        name="project",
    )(*blocks, distant(out_proj.T))


def of_core(parity, table, chip, mine_ref, other_ref):
    mine = mine_ref[table[chip]].astype(f32)
    other = other_ref[table[CHIPS + chip]].astype(f32)
    return jnp.where(this_core() == parity, mine, other)


def slot_masks(mark, rows):
    lane = lax.broadcasted_iota(jnp.int32, (2 * rows, 128), 1)
    wanted = (lane % CAP + 1).astype(f32)
    second = lax.broadcasted_iota(jnp.int32, (2 * rows, 128), 0) >= rows
    right_half = (lane % (2 * CAP) >= CAP) == second
    return jnp.where((mark == wanted) & right_half, 1.0, 0.0).astype(bf16)


def gate_kernel(table, places_ref, places_other, levels_ref, levels_other, out_ref, made_ref):
    dp = lax.axis_index("dp")
    group = dp // EPG
    rows = places_ref.shape[1]
    lane = lax.broadcasted_iota(jnp.int32, (2 * rows, 128), 1)
    for quarter in range(CHIPS // QUARTER):
        for parity in range(CORES):
            for pair in range(QUARTER // 2):
                chips = (quarter * QUARTER + 2 * pair, quarter * QUARTER + 2 * pair + 1)
                mark = jnp.concatenate(
                    [of_core(parity, table, chip, places_ref, places_other) for chip in chips]
                )
                level = jnp.concatenate(
                    [of_core(parity, table, chip, levels_ref, levels_other) for chip in chips]
                )
                total = jnp.sum(jnp.where(lane < GROUPS * EPG, level, 0.0), axis=1, keepdims=True)
                mine = jnp.sum(jnp.where(lane == dp, level, 0.0), axis=1, keepdims=True)
                home = jnp.sum(
                    jnp.where(lane == GROUPS * EPG + group, level, 0.0), axis=1, keepdims=True
                )
                gate = route_scale * mine / total
                high = gate.astype(bf16).astype(f32)
                values = jnp.where(lane == 0, high, jnp.where(lane == 1, gate - high, 0.0))
                values = jnp.where(lane == 2, home, values).astype(bf16)
                made_ref[...] = lax.dot_general(
                    slot_masks(mark, rows), values, (((0,), (0,)), ((), ())),
                    preferred_element_type=f32,
                )
                to = quarter * CORES * PART + parity * PART + pair * 2 * CAP
                out_ref[to : to + 2 * CAP] = made_ref[
                    pl.ds(pl.multiple_of(group * 2 * CAP, 2 * CAP), 2 * CAP)
                ]


def gate_table(table, places, levels):
    whole = pl.BlockSpec(memory_space=pltpu.VMEM)
    return pl.pallas_call(
        gate_kernel,
        in_specs=[pl.BlockSpec(memory_space=pltpu.SMEM)] + [whole] * 4,
        out_specs=whole,
        out_shape=jax.ShapeDtypeStruct((CHIPS * CORES * CAP, 128), f32),
        scratch_shapes=[pltpu.VMEM((128, 128), f32)],
        compiler_params=pltpu.CompilerParams(vmem_limit_bytes=VMEM),
        cost_estimate=pl.CostEstimate(flops=10**8, bytes_accessed=10**6, transcendentals=0),
        name="gate_table",
    )(table, *[distant(value) for value in (*places, *levels)])


def select_kernel(table, sums_ref, sums_other, res_ref, places_ref, places_other, out_ref):
    rows = res_ref.shape[2]

    for parity in range(CORES):
        for pair in range(QUARTER // 2):
            quarters = []
            for quarter in range(CHIPS // QUARTER):
                parts = []
                marks = []
                for chip in (quarter * QUARTER + 2 * pair, quarter * QUARTER + 2 * pair + 1):
                    attention = of_core(parity, table, chip, sums_ref, sums_other)
                    parts.append((res_ref[chip, parity].astype(f32) + attention).astype(bf16))
                    marks.append(of_core(parity, table, chip, places_ref, places_other))
                hidden = jnp.concatenate(parts, axis=0)
                mark = jnp.concatenate(marks, axis=0)
                pick = slot_masks(mark, rows)
                quarters.append(
                    lax.dot_general(
                        pick, hidden, (((0,), (0,)), ((), ())), preferred_element_type=f32
                    )
                )
            chosen = jnp.concatenate(quarters, axis=1).astype(bf16)
            at = parity * PART + pair * 2 * CAP
            for group in range(GROUPS):
                block = chosen[group * 2 * CAP : (group + 1) * 2 * CAP]
                out_ref[2 * group, at : at + 2 * CAP, :] = block
                out_ref[2 * group + 1, at : at + 2 * CAP, :] = block


def select(table, parts, residual, places):
    columns = residual.shape[-1]
    whole = pl.BlockSpec(memory_space=pltpu.VMEM)
    return pl.pallas_call(
        select_kernel,
        in_specs=[pl.BlockSpec(memory_space=pltpu.SMEM)] + [whole] * 5,
        out_specs=whole,
        out_shape=jax.ShapeDtypeStruct(
            (CHIPS, CORES * PART, CHIPS // QUARTER * columns), bf16
        ),
        compiler_params=pltpu.CompilerParams(vmem_limit_bytes=VMEM),
        cost_estimate=pl.CostEstimate(flops=10**9, bytes_accessed=6 * 10**6, transcendentals=0),
        name="select",
    )(table, *parts, distant(residual), *[distant(value) for value in places])


def unpacked(block, columns):
    parts = [block[:, q * columns : (q + 1) * columns] for q in range(CHIPS // QUARTER)]
    return jnp.concatenate(parts, axis=0)


def weight_copies(gw_hbm, uw_hbm, w_ref, sems, core):
    units = gw_hbm.shape[-1]
    span = CHIPS // QUARTER
    copies = []
    for part in range(QUARTER):
        chips = pl.ds(part * span, span)
        for n, source in enumerate((gw_hbm, uw_hbm)):
            lanes = slice(n * units, (n + 1) * units)
            copies.append(
                pltpu.make_async_copy(
                    source.at[chips, core], w_ref.at[chips, :, lanes], sems.at[part, n]
                )
            )
    return copies


def raise_up(x_ref, w_ref, acc, copies=None):
    span = CHIPS // QUARTER
    for chip in range(CHIPS):
        if copies is not None and chip % span == 0:
            copies[chip // span * 2].wait()
            copies[chip // span * 2 + 1].wait()
        acc = acc + jnp.dot(
            unpacked(x_ref[chip], w_ref.shape[1]), w_ref[chip], preferred_element_type=f32
        )
    return acc


def up_kernel(x_ref, gw_hbm, uw_hbm, acc_ref, next_ref, w_ref, sems, next_sems):
    core = this_core()
    copies = weight_copies(gw_hbm, uw_hbm, w_ref, sems, core)
    following = weight_copies(gw_hbm, uw_hbm, next_ref, next_sems, 1 - core)
    for copy in copies + following:
        copy.start()
    acc_ref[...] = raise_up(x_ref, w_ref, jnp.zeros(acc_ref.shape, f32), copies)
    for copy in following:
        copy.wait()


def up(x, gate_weight, up_weight):
    columns, units = gate_weight.shape[2:]
    slots = x.shape[1] * CHIPS // QUARTER
    whole = pl.BlockSpec(memory_space=pltpu.VMEM)
    far = pl.BlockSpec(memory_space=pltpu.HBM)
    return pl.pallas_call(
        up_kernel,
        in_specs=[whole, far, far],
        out_specs=(whole, whole),
        out_shape=(
            jax.ShapeDtypeStruct((slots, 2 * units), f32),
            pltpu.VMEM((CHIPS, columns, 2 * units), bf16),
        ),
        scratch_shapes=[
            pltpu.VMEM((CHIPS, columns, 2 * units), bf16),
            pltpu.SemaphoreType.DMA((QUARTER, 2)),
            pltpu.SemaphoreType.DMA((QUARTER, 2)),
        ],
        compiler_params=pltpu.CompilerParams(vmem_limit_bytes=VMEM),
        cost_estimate=pl.CostEstimate(
            flops=4 * CHIPS * slots * columns * units, bytes_accessed=9 * 10**6, transcendentals=0
        ),
        name="up",
    )(x, distant(gate_weight), distant(up_weight))


def act_kernel(acc_ref, x_ref, w_ref, act_ref):
    acc = raise_up(x_ref, w_ref, acc_ref[...])
    units = act_ref.shape[1]
    gated = acc[:, :units]
    act_ref[...] = (gated / (1.0 + jnp.exp(-gated)) * acc[:, units:]).astype(bf16)


def activate(acc, x, weight):
    slots = acc.shape[0]
    units = weight.shape[-1] // 2
    whole = pl.BlockSpec(memory_space=pltpu.VMEM)
    return pl.pallas_call(
        act_kernel,
        in_specs=[whole] * 3,
        out_specs=whole,
        out_shape=jax.ShapeDtypeStruct((slots, units), bf16),
        compiler_params=pltpu.CompilerParams(vmem_limit_bytes=VMEM),
        cost_estimate=pl.CostEstimate(
            flops=4 * slots * units * weight.shape[0] * weight.shape[1],
            bytes_accessed=6 * 10**6,
            transcendentals=slots * units,
        ),
        name="activate",
    )(acc, x, weight)


def cut_kernel(w_hbm, out_ref):
    pltpu.sync_copy(w_hbm.at[:, quarter_lanes(2, out_ref.shape[1])], out_ref)


def cut(down_weight):
    units, width = down_weight.shape
    return pl.pallas_call(
        cut_kernel,
        in_specs=[pl.BlockSpec(memory_space=pltpu.HBM)],
        out_specs=pl.BlockSpec(memory_space=pltpu.VMEM),
        out_shape=jax.ShapeDtypeStruct((units, width // PLANES), bf16),
        compiler_params=pltpu.CompilerParams(vmem_limit_bytes=VMEM),
        cost_estimate=pl.CostEstimate(flops=0, bytes_accessed=2 * 10**6, transcendentals=0),
        name="cut",
    )(distant(down_weight))


def down_kernel(a0, a1, a2, a3, own_hbm, w1, w2, w3, gates_ref, out_ref, w_ref, sems):
    acts = (a0, a1, a2, a3)
    z = lax.axis_index("tensor")
    units = a0.shape[1]
    width = out_ref.shape[1]
    lanes = pl.ds(pl.multiple_of(z * width, width), width)
    copies = [
        pltpu.make_async_copy(source, w_ref.at[n * units : (n + 1) * units], sems.at[n])
        for n, source in enumerate((own_hbm.at[:, lanes], w1, w2, w3))
    ]
    for copy in copies:
        copy.start()
    gate = gates_ref[:, 0:1] + gates_ref[:, 1:2]
    left = jnp.concatenate([act[...] for act in acts], axis=1)
    for copy in copies:
        copy.wait()
    block = 256
    for at in range(0, width, block):
        made = jnp.dot(left, w_ref[:, at : at + block], preferred_element_type=f32)
        out_ref[:, at : at + block] = (made * gate).astype(bf16)


def down(acts, own_weight, weights, gates):
    slots = acts[0].shape[0]
    units, width = weights[0].shape
    whole = pl.BlockSpec(memory_space=pltpu.VMEM)
    far = pl.BlockSpec(memory_space=pltpu.HBM)
    return pl.pallas_call(
        down_kernel,
        in_specs=[whole] * 4 + [far] * 4 + [whole],
        out_specs=whole,
        out_shape=jax.ShapeDtypeStruct((slots, width), bf16),
        scratch_shapes=[
            pltpu.VMEM((PLANES * units, width), bf16),
            pltpu.SemaphoreType.DMA((PLANES,)),
        ],
        compiler_params=pltpu.CompilerParams(vmem_limit_bytes=VMEM),
        cost_estimate=pl.CostEstimate(
            flops=8 * slots * units * width, bytes_accessed=6 * 10**6, transcendentals=0
        ),
        name="down",
    )(*acts, distant(own_weight), *[distant(weight) for weight in weights], gates)


def join_kernel(y_ref, received_ref, own_hbm, other_hbm, gates_ref, out_ref, x_ref, sems):
    half, width = out_ref.shape
    columns = own_hbm.shape[2] // (CHIPS // QUARTER)
    dp, z = lax.axis_index("dp"), lax.axis_index("tensor")
    core = dp % CORES
    step_here = dp // CORES % 2
    chips = QUARTER // 2
    near = pl.ds(z * QUARTER + step_here * chips, chips)
    rows = pl.ds(pl.multiple_of(core * PART, PART), PART)
    copies = [
        pltpu.make_async_copy(source.at[near, rows], x_ref.at[n], sems.at[n])
        for n, source in enumerate((own_hbm, other_hbm))
    ]
    for copy in copies:
        copy.start()
    both, homes = [], []
    for q in range(CHIPS // QUARTER):
        at = pl.ds(pl.multiple_of(q * CORES * PART + core * PART, PART), PART)
        both.append(y_ref[at, :].astype(f32) + received_ref[q * PART : (q + 1) * PART, :].astype(f32))
        homes.append(gates_ref[at, 2:3])
    total = jnp.concatenate(both, axis=0)
    home = jnp.concatenate(homes, axis=0)
    out_ref[...] = total.astype(bf16)
    for copy in copies:
        copy.wait()
    block = chips * CORES * columns
    flip = core == 1
    parts = []
    for chip in range(chips):
        mine = unpacked(x_ref[0, chip].astype(f32), columns)
        theirs = unpacked(x_ref[1, chip].astype(f32), columns)
        parts.append(jnp.where(flip, theirs, mine))
        parts.append(jnp.where(flip, mine, theirs))
    hidden = jnp.concatenate(parts, axis=1) * home
    for step in range(width // block):

        @pl.when(step_here == step)
        def _():
            at = slice(step * block, (step + 1) * block)
            out_ref[:, at] = (total[:, at] + hidden).astype(bf16)


def join(y, received, own, other, gates):
    whole = pl.BlockSpec(memory_space=pltpu.VMEM)
    far = pl.BlockSpec(memory_space=pltpu.HBM)
    return pl.pallas_call(
        join_kernel,
        in_specs=[whole, whole, far, far, whole],
        out_specs=whole,
        out_shape=jax.ShapeDtypeStruct(received.shape, bf16),
        scratch_shapes=[
            pltpu.VMEM((2, QUARTER // 2, PART, own.shape[2]), bf16),
            pltpu.SemaphoreType.DMA((2,)),
        ],
        compiler_params=pltpu.CompilerParams(vmem_limit_bytes=VMEM),
        cost_estimate=pl.CostEstimate(flops=10**6, bytes_accessed=2 * 10**6, transcendentals=0),
        name="join",
    )(y, received, own, other, gates)


def around(value, x_core):
    return [value] + [move_ring(value, by, x_core) for by in (1, 3, 2)]


def local(
    residual,
    query_latent,
    query_rope,
    cache_latent,
    cache_rope,
    lengths,
    value_up,
    out_proj,
    gate_proj,
    up_proj,
    down_proj,
    groups,
    expert_picks,
    gate_levels,
):
    rows, model = residual.shape
    columns = out_proj.shape[1]
    dp = lax.axis_index("dp")
    z = lax.axis_index("tensor")
    core = dp % CORES
    chip = dp // CORES
    here_x, here_y = chip // SIDE, chip % SIDE

    quarter = model // PLANES
    opposite = move_z(cut(down_proj[0]), 2)

    flat, places_here, spread, *sent = attend(
        query_latent, query_rope, cache_latent, cache_rope, lengths, value_up, down_proj[0], residual, columns,
        (groups.T, expert_picks.T, gate_levels.T),
    )
    weighting = places_here == (jnp.arange(128) % CAP + 1).astype(bf16)
    weighting = weighting.astype(bf16)

    blocks = jnp.concatenate(around(flat, 0), axis=0)

    spread, blocks, opposite = lax.optimization_barrier((spread, blocks, opposite))
    residual_columns = lax.all_to_all(spread, "dp", split_axis=0, concat_axis=0, tiled=True)
    downs = [move_z(part, by) for part, by in zip(sent, (1, 3))] + [opposite]
    residual_columns = residual_columns.reshape(CHIPS, CORES, rows, columns)

    blocks = around(blocks, 1)
    blocks[3], downs[:2], residual_columns = lax.optimization_barrier(
        (blocks[3], downs[:2], residual_columns)
    )
    swapped = [move_core(block) for block in blocks]
    mine, places_mine, levels_mine = project(blocks, out_proj)
    theirs, places_theirs, levels_theirs = project(swapped, out_proj)
    mine, theirs = sum_z(mine, theirs)
    places, levels = (places_mine, places_theirs), (levels_mine, levels_theirs)

    far = jnp.arange(SIDE, dtype=jnp.int32)
    x_far = (here_x - far) % SIDE
    y_far = (here_y - far) % SIDE
    x_spot = (x_far ^ (x_far >> 1))[:, None]
    y_spot = (y_far ^ (y_far >> 1))[None, :]
    x_first = (y_spot * SIDE + x_spot).reshape(CHIPS)
    y_first = (x_spot * SIDE + y_spot).reshape(CHIPS)
    table = jnp.where(
        core == 0, jnp.concatenate([x_first, y_first]), jnp.concatenate([y_first, x_first])
    ).astype(jnp.int32)
    gates = gate_table(table, places, levels)
    outgoing = select(table, (mine, theirs), residual_columns, places)
    outgoing, gates = lax.optimization_barrier((outgoing, gates))

    own = chip_exchange(outgoing)
    other = move_core(own)
    gate_weight = gate_proj.reshape(CHIPS, CORES, columns, -1)
    up_weight = up_proj.reshape(CHIPS, CORES, columns, -1)
    acc, weight = up(own, gate_weight, up_weight)
    act = activate(acc, other, weight)
    acts = [act] + [move_z(act, by) for by in (1, 3, 2)]
    made = down(acts, down_proj[0], downs, gates)
    pieces = made.reshape(CHIPS // QUARTER, CORES, PART, quarter)
    theirs = lax.dynamic_index_in_dim(pieces, 1 - core, 1, keepdims=False)
    received = move_core(theirs.reshape(CHIPS * CAP, quarter))
    returning = join(made, received, own, other, gates)
    returning = returning.reshape(CHIPS, CAP, quarter)
    returning, weighting = lax.optimization_barrier((returning, weighting))

    returned = chip_exchange(returning).reshape(CHIPS * CAP, quarter)
    mixed = jnp.dot(weighting, returned, preferred_element_type=f32).astype(bf16)
    return spread_z(mixed).transpose(1, 0, 2).reshape(rows, model)


def solution(mesh):
    return jax.shard_map(
        local,
        mesh=mesh,
        in_specs=(
            P("dp", None),
            P("dp", "tensor", None),
            P("dp", "tensor", None),
            P("dp", None, None),
            P("dp", None, None),
            P("dp"),
            P("tensor", None, None),
            P("tensor", "dp"),
            P("dp", None, "tensor"),
            P("dp", None, "tensor"),
            P("dp", "tensor", None),
            P("dp", None),
            P("dp", None),
            P("dp", None),
        ),
        out_specs=P("dp", None),
        check_vma=False,
    )
```

```python
import jax
import jax.numpy as jnp
from jax import lax
from jax.experimental import pallas as pl
from jax.experimental.pallas import tpu as pltpu
from jax.sharding import PartitionSpec as P

SIDE = 4
CORES = 2
CHIPS = SIDE * SIDE
PLANES = 4
TOPG = 4
GROUPS = 8
EPG = 4
CAP = 8
QUARTER = 4
PART = QUARTER * CAP

score_scale = 192.0 ** (-0.5)
route_scale = 2.5
far_below = -1e30

f32 = jnp.float32
bf16 = jnp.bfloat16
VMEM = 28 * 1024 * 1024


def distant(value):
    return pltpu.with_memory_space_constraint(value, pltpu.HBM)


def dp_index(x, y, c):
    return (x * SIDE + y) * CORES + c


def place_pairs(place):
    return [
        (dp_index(x, y, c), dp_index(*place(x, y, c)))
        for x in range(SIDE)
        for y in range(SIDE)
        for c in range(CORES)
    ]


def move_core(value):
    return lax.ppermute(value, "dp", place_pairs(lambda x, y, c: (x, y, 1 - c)))


def move_ring(value, by, x_core):
    def place(x, y, c):
        return ((x + by) % SIDE, y, c) if c == x_core else (x, (y + by) % SIDE, c)

    return lax.ppermute(value, "dp", place_pairs(place))


def move_z(value, by):
    return lax.ppermute(value, "tensor", [(z, (z + by) % PLANES) for z in range(PLANES)])


def spread_z(value):
    copies = jnp.broadcast_to(value[None], (PLANES,) + value.shape)
    return lax.all_to_all(copies, "tensor", split_axis=0, concat_axis=0, tiled=True)


def sum_z(low, high):
    def add(block, mask):
        pairs = [(z, z ^ mask) for z in range(PLANES)]
        moved = lax.ppermute(block, "tensor", pairs)
        return (block.astype(f32) + moved.astype(f32)).astype(bf16)

    low, high = add(low, 1), add(high, 3)
    low, high = add(low, 3), add(high, 1)
    return low, high


def chip_exchange(value):
    groups = [[dp_index(x, y, c) for x in range(SIDE) for y in range(SIDE)] for c in range(CORES)]
    return lax.all_to_all(
        value, "dp", split_axis=0, concat_axis=0, axis_index_groups=groups, tiled=True
    )


DEPTH = 6


def this_core():
    return lax.axis_index("dp") % CORES


def quarter_lanes(by, width):
    z = lax.axis_index("tensor")
    return pl.ds(pl.multiple_of((z + by) % PLANES * width, width), width)


def upright(ref):
    rows = ref.shape[1]
    same = lax.broadcasted_iota(jnp.int32, (rows, rows), 0) == lax.broadcasted_iota(
        jnp.int32, (rows, rows), 1
    )
    turned = lax.dot_general(
        jnp.where(same, 1.0, 0.0).astype(bf16),
        ref[...].astype(f32).astype(bf16),
        (((1,), (1,)), ((), ())),
        preferred_element_type=f32,
    )
    return turned.astype(jnp.int32)


def route_tables(groups, picks, levels):
    rows = groups.shape[0]
    lane = lax.broadcasted_iota(jnp.int32, (rows, 128), 1)
    member = lane < 0
    for t in range(TOPG):
        member = member | (lane // 16 == groups[:, t : t + 1])
    below = lax.broadcasted_iota(jnp.int32, (rows, rows), 0) >= lax.broadcasted_iota(
        jnp.int32, (rows, rows), 1
    )
    counted = jnp.dot(
        jnp.where(below, 1.0, 0.0).astype(bf16),
        jnp.where(member, 1.0, 0.0).astype(bf16),
        preferred_element_type=f32,
    )
    places = jnp.where(member, counted, 0.0)
    table = jnp.where(lane - GROUPS * EPG == groups[:, :1], 1, 0)
    for k in range(picks.shape[1]):
        pick = picks[:, k : k + 1]
        group = jnp.zeros_like(pick)
        for t in range(TOPG):
            group = jnp.where(pick // EPG == t, groups[:, t : t + 1], group)
        table = jnp.where(lane == group * EPG + pick % EPG, levels[:, k : k + 1], table)
    return places.astype(bf16), table.astype(f32).astype(bf16)


def attend_kernel(
    lengths, q_ref, qr_ref, k_hbm, r_hbm, vu_hbm, dw_hbm, res_ref, groups_ref, picks_ref, levels_ref,
    out_ref, places_ref, spread_ref, cut_1, cut_3,
    k_ref, r_ref, mix_ref, vu_ref, cut_ref, sems, cut_sems, vu_sem,
):
    rows, heads, lat = q_ref.shape
    width = vu_ref.shape[2]
    cuts = (cut_1, cut_3)
    vu_copy = pltpu.make_async_copy(vu_hbm, vu_ref, vu_sem)

    def copies(row, slot):
        return (
            pltpu.make_async_copy(k_hbm.at[row], k_ref.at[slot], sems.at[0, slot]),
            pltpu.make_async_copy(r_hbm.at[row], r_ref.at[slot], sems.at[1, slot]),
        )

    entering, leaving = [], []
    for n, by in enumerate((1, 3)):
        lanes = quarter_lanes(by, cut_ref.shape[2])
        entering.append(pltpu.make_async_copy(dw_hbm.at[:, lanes], cut_ref.at[n], cut_sems.at[0, n]))
        leaving.append(pltpu.make_async_copy(cut_ref.at[n], cuts[n], cut_sems.at[1, n]))
    for row in range(DEPTH):
        for copy in copies(row, row):
            copy.start()
    for copy in entering:
        copy.start()
    vu_copy.start()

    columns = spread_ref.shape[2]
    for j in range(spread_ref.shape[0]):
        spread_ref[j] = res_ref[:, j * columns : (j + 1) * columns]
    places, levels = route_tables(upright(groups_ref), upright(picks_ref), upright(levels_ref))
    places_ref[...] = places
    out_ref[:, heads * width : heads * width + 128] = places
    out_ref[:, heads * width + 128 :] = levels

    def scores_of(row, slot):
        scores = lax.dot_general(
            q_ref[row], k_ref[slot], (((1,), (1,)), ((), ())), preferred_element_type=f32
        )
        return scores + jnp.dot(qr_ref[row], r_ref[slot], preferred_element_type=f32)

    def weights_of(scores, row):
        scores = scores * score_scale
        place = lax.broadcasted_iota(jnp.int32, scores.shape, 1)
        scores = jnp.where(place < lengths[row], scores, far_below)
        highest = jnp.max(scores, axis=1, keepdims=True)
        raised = jnp.exp(scores - highest)
        return (raised * (1.0 / jnp.sum(raised, axis=1, keepdims=True))).astype(bf16)

    def finish(scores, row, slot):
        mix = jnp.dot(weights_of(scores, row), k_ref[slot], preferred_element_type=f32)
        at = pl.ds(row * heads, heads)
        for j in range(mix_ref.shape[0]):
            mix_ref[j, at, :] = mix[:, j * 128 : (j + 1) * 128]

    def wait(row, slot):
        for copy in copies(row, slot):
            copy.wait()

    scored, weighed = {}, {}
    for row in range(rows + 2):
        if row < rows:
            wait(row, row % DEPTH)
            scored[row] = scores_of(row, row % DEPTH)
        if 0 <= row - 1 < rows:
            weighed[row - 1] = weights_of(scored.pop(row - 1), row - 1)
        if row >= 2:
            done = row - 2
            mix = jnp.dot(weighed.pop(done), k_ref[done % DEPTH], preferred_element_type=f32)
            at = pl.ds(done * heads, heads)
            for j in range(mix_ref.shape[0]):
                mix_ref[j, at, :] = mix[:, j * 128 : (j + 1) * 128]
            if done + DEPTH < rows:
                for copy in copies(done + DEPTH, done % DEPTH):
                    copy.start()
        if row == DEPTH:
            for n, copy in enumerate(entering):
                copy.wait()
                leaving[n].start()
    vu_copy.wait()
    for h in range(heads):
        left = [mix_ref[j, pl.ds(h, rows, stride=heads), :] for j in range(mix_ref.shape[0])]
        left = jnp.concatenate(left, axis=1).astype(bf16)
        out_ref[:, h * width : (h + 1) * width] = jnp.dot(
            left, vu_ref[h], preferred_element_type=f32
        ).astype(bf16)
    for copy in leaving:
        copy.wait()


def attend(
    query_latent, query_rope, cache_latent, cache_rope, lengths, value_up, down_weight, residual, columns, routing
):
    rows, heads, lat = query_latent.shape
    rope = query_rope.shape[2]
    positions = cache_latent.shape[1]
    width = value_up.shape[2]
    units, model = down_weight.shape
    whole = pl.BlockSpec(memory_space=pltpu.VMEM)
    small = pl.BlockSpec(memory_space=pltpu.SMEM)
    far = pl.BlockSpec(memory_space=pltpu.HBM)
    return pl.pallas_call(
        attend_kernel,
        in_specs=[small, whole, whole] + [far] * 4 + [whole] * 4,
        out_specs=(whole,) * 3 + (far,) * 2,
        out_shape=(
            jax.ShapeDtypeStruct((rows, heads * width + 2 * 128), bf16),
            jax.ShapeDtypeStruct((rows, 128), bf16),
            jax.ShapeDtypeStruct((residual.shape[1] // columns, rows, columns), bf16),
        )
        + (jax.ShapeDtypeStruct((units, model // PLANES), bf16),) * 2,
        scratch_shapes=[
            pltpu.VMEM((DEPTH, positions, lat), bf16),
            pltpu.VMEM((DEPTH, rope, positions), bf16),
            pltpu.VMEM((lat // 128, (rows + 1) * heads, 128), f32),
            pltpu.VMEM((heads, lat, width), bf16),
            pltpu.VMEM((2, units, model // PLANES), bf16),
            pltpu.SemaphoreType.DMA((2, DEPTH)),
            pltpu.SemaphoreType.DMA((2, 2)),
            pltpu.SemaphoreType.DMA,
        ],
        compiler_params=pltpu.CompilerParams(vmem_limit_bytes=VMEM),
        cost_estimate=pl.CostEstimate(
            flops=4 * rows * heads * positions * lat,
            bytes_accessed=2 * rows * positions * (lat + rope),
            transcendentals=rows * heads * positions,
        ),
        name="attend",
    )(
        lengths, query_latent, query_rope, distant(cache_latent), distant(cache_rope), distant(value_up),
        distant(down_weight), residual, *routing,
    )


def project_kernel(*refs):
    blocks, w_hbm = refs[:SIDE], refs[SIDE]
    out_ref, places_ref, levels_ref, w_ref, b_ref, sems = refs[SIDE + 1 :]
    depth = w_ref.shape[1]
    copy = pltpu.make_async_copy(w_hbm, w_ref, sems.at[SIDE])
    moves = [
        pltpu.make_async_copy(block, b_ref.at[n], sems.at[n]) for n, block in enumerate(blocks)
    ]
    for move in moves:
        move.start()
    copy.start()
    for move in moves:
        move.wait()
    blocks = [b_ref.at[n] for n in range(SIDE)]
    left = jnp.concatenate([block[:, :depth] for block in blocks])
    rows = out_ref.shape[1]
    for i, block in enumerate(blocks):
        for j in range(SIDE):
            at = slice(j * rows, (j + 1) * rows)
            places_ref[i * SIDE + j] = block[at, depth : depth + 128]
            levels_ref[i * SIDE + j] = block[at, depth + 128 :]
    copy.wait()
    made = lax.dot_general(left, w_ref[...], (((1,), (1,)), ((), ())), preferred_element_type=f32)
    made = made.astype(bf16)
    for n in range(CHIPS):
        out_ref[n] = made[n * rows : (n + 1) * rows]


def project(blocks, out_proj):
    depth, columns = out_proj.shape
    rows = blocks[0].shape[0] // SIDE
    whole = pl.BlockSpec(memory_space=pltpu.VMEM)
    far = pl.BlockSpec(memory_space=pltpu.HBM)
    table = pltpu.HBM((CHIPS, rows, 128), bf16)
    return pl.pallas_call(
        project_kernel,
        in_specs=[far] * (SIDE + 1),
        out_specs=(whole,) * 3,
        out_shape=(jax.ShapeDtypeStruct((CHIPS, rows, columns), bf16), table, table),
        scratch_shapes=[
            pltpu.VMEM((columns, depth), bf16),
            pltpu.VMEM((SIDE,) + blocks[0].shape, bf16),
            pltpu.SemaphoreType.DMA((SIDE + 1,)),
        ],
        compiler_params=pltpu.CompilerParams(vmem_limit_bytes=VMEM),
        cost_estimate=pl.CostEstimate(flops=5 * 10**8, bytes_accessed=4 * 10**6, transcendentals=0),
        name="project",
    )(*blocks, distant(out_proj.T))


def of_core(parity, table, chip, mine_ref, other_ref):
    mine = mine_ref[table[chip]].astype(f32)
    other = other_ref[table[CHIPS + chip]].astype(f32)
    return jnp.where(this_core() == parity, mine, other)


def slot_masks(mark, rows):
    lane = lax.broadcasted_iota(jnp.int32, (2 * rows, 128), 1)
    wanted = (lane % CAP + 1).astype(f32)
    second = lax.broadcasted_iota(jnp.int32, (2 * rows, 128), 0) >= rows
    right_half = (lane % (2 * CAP) >= CAP) == second
    return jnp.where((mark == wanted) & right_half, 1.0, 0.0).astype(bf16)


def gate_kernel(table, places_ref, places_other, levels_ref, levels_other, out_ref, made_ref):
    dp = lax.axis_index("dp")
    group = dp // EPG
    rows = places_ref.shape[1]
    lane = lax.broadcasted_iota(jnp.int32, (2 * rows, 128), 1)
    for quarter in range(CHIPS // QUARTER):
        for parity in range(CORES):
            for pair in range(QUARTER // 2):
                chips = (quarter * QUARTER + 2 * pair, quarter * QUARTER + 2 * pair + 1)
                mark = jnp.concatenate(
                    [of_core(parity, table, chip, places_ref, places_other) for chip in chips]
                )
                level = jnp.concatenate(
                    [of_core(parity, table, chip, levels_ref, levels_other) for chip in chips]
                )
                total = jnp.sum(jnp.where(lane < GROUPS * EPG, level, 0.0), axis=1, keepdims=True)
                mine = jnp.sum(jnp.where(lane == dp, level, 0.0), axis=1, keepdims=True)
                home = jnp.sum(
                    jnp.where(lane == GROUPS * EPG + group, level, 0.0), axis=1, keepdims=True
                )
                gate = route_scale * mine / total
                high = gate.astype(bf16).astype(f32)
                values = jnp.where(lane == 0, high, jnp.where(lane == 1, gate - high, 0.0))
                values = jnp.where(lane == 2, home, values).astype(bf16)
                made_ref[...] = lax.dot_general(
                    slot_masks(mark, rows), values, (((0,), (0,)), ((), ())),
                    preferred_element_type=f32,
                )
                to = quarter * CORES * PART + parity * PART + pair * 2 * CAP
                out_ref[to : to + 2 * CAP] = made_ref[
                    pl.ds(pl.multiple_of(group * 2 * CAP, 2 * CAP), 2 * CAP)
                ]


def gate_table(table, places, levels):
    whole = pl.BlockSpec(memory_space=pltpu.VMEM)
    return pl.pallas_call(
        gate_kernel,
        in_specs=[pl.BlockSpec(memory_space=pltpu.SMEM)] + [whole] * 4,
        out_specs=whole,
        out_shape=jax.ShapeDtypeStruct((CHIPS * CORES * CAP, 128), f32),
        scratch_shapes=[pltpu.VMEM((128, 128), f32)],
        compiler_params=pltpu.CompilerParams(vmem_limit_bytes=VMEM),
        cost_estimate=pl.CostEstimate(flops=10**8, bytes_accessed=10**6, transcendentals=0),
        name="gate_table",
    )(table, *[distant(value) for value in (*places, *levels)])


def select_kernel(table, sums_ref, sums_other, res_ref, places_ref, places_other, out_ref):
    rows = res_ref.shape[2]

    for parity in range(CORES):
        for pair in range(QUARTER // 2):
            quarters = []
            for quarter in range(CHIPS // QUARTER):
                parts = []
                marks = []
                for chip in (quarter * QUARTER + 2 * pair, quarter * QUARTER + 2 * pair + 1):
                    attention = of_core(parity, table, chip, sums_ref, sums_other)
                    parts.append((res_ref[chip, parity].astype(f32) + attention).astype(bf16))
                    marks.append(of_core(parity, table, chip, places_ref, places_other))
                hidden = jnp.concatenate(parts, axis=0)
                mark = jnp.concatenate(marks, axis=0)
                pick = slot_masks(mark, rows)
                quarters.append(
                    lax.dot_general(
                        pick, hidden, (((0,), (0,)), ((), ())), preferred_element_type=f32
                    )
                )
            chosen = jnp.concatenate(quarters, axis=1).astype(bf16)
            at = parity * PART + pair * 2 * CAP
            for group in range(GROUPS):
                block = chosen[group * 2 * CAP : (group + 1) * 2 * CAP]
                out_ref[2 * group, at : at + 2 * CAP, :] = block
                out_ref[2 * group + 1, at : at + 2 * CAP, :] = block


def select(table, parts, residual, places):
    columns = residual.shape[-1]
    whole = pl.BlockSpec(memory_space=pltpu.VMEM)
    return pl.pallas_call(
        select_kernel,
        in_specs=[pl.BlockSpec(memory_space=pltpu.SMEM)] + [whole] * 5,
        out_specs=whole,
        out_shape=jax.ShapeDtypeStruct(
            (CHIPS, CORES * PART, CHIPS // QUARTER * columns), bf16
        ),
        compiler_params=pltpu.CompilerParams(vmem_limit_bytes=VMEM),
        cost_estimate=pl.CostEstimate(flops=10**9, bytes_accessed=6 * 10**6, transcendentals=0),
        name="select",
    )(table, *parts, distant(residual), *[distant(value) for value in places])


def unpacked(block, columns):
    parts = [block[:, q * columns : (q + 1) * columns] for q in range(CHIPS // QUARTER)]
    return jnp.concatenate(parts, axis=0)


def weight_copies(gw_hbm, uw_hbm, w_ref, sems, core):
    units = gw_hbm.shape[-1]
    span = CHIPS // QUARTER
    copies = []
    for part in range(QUARTER):
        chips = pl.ds(part * span, span)
        for n, source in enumerate((gw_hbm, uw_hbm)):
            lanes = slice(n * units, (n + 1) * units)
            copies.append(
                pltpu.make_async_copy(
                    source.at[chips, core], w_ref.at[chips, :, lanes], sems.at[part, n]
                )
            )
    return copies


def raise_up(x_ref, w_ref, acc, copies=None):
    span = CHIPS // QUARTER
    for chip in range(CHIPS):
        if copies is not None and chip % span == 0:
            copies[chip // span * 2].wait()
            copies[chip // span * 2 + 1].wait()
        acc = acc + jnp.dot(
            unpacked(x_ref[chip], w_ref.shape[1]), w_ref[chip], preferred_element_type=f32
        )
    return acc


def up_kernel(x_ref, gw_hbm, uw_hbm, acc_ref, next_ref, w_ref, sems, next_sems):
    core = this_core()
    copies = weight_copies(gw_hbm, uw_hbm, w_ref, sems, core)
    following = weight_copies(gw_hbm, uw_hbm, next_ref, next_sems, 1 - core)
    for copy in copies + following:
        copy.start()
    acc_ref[...] = raise_up(x_ref, w_ref, jnp.zeros(acc_ref.shape, f32), copies)
    for copy in following:
        copy.wait()


def up(x, gate_weight, up_weight):
    columns, units = gate_weight.shape[2:]
    slots = x.shape[1] * CHIPS // QUARTER
    whole = pl.BlockSpec(memory_space=pltpu.VMEM)
    far = pl.BlockSpec(memory_space=pltpu.HBM)
    return pl.pallas_call(
        up_kernel,
        in_specs=[whole, far, far],
        out_specs=(whole, whole),
        out_shape=(
            jax.ShapeDtypeStruct((slots, 2 * units), f32),
            pltpu.VMEM((CHIPS, columns, 2 * units), bf16),
        ),
        scratch_shapes=[
            pltpu.VMEM((CHIPS, columns, 2 * units), bf16),
            pltpu.SemaphoreType.DMA((QUARTER, 2)),
            pltpu.SemaphoreType.DMA((QUARTER, 2)),
        ],
        compiler_params=pltpu.CompilerParams(vmem_limit_bytes=VMEM),
        cost_estimate=pl.CostEstimate(
            flops=4 * CHIPS * slots * columns * units, bytes_accessed=9 * 10**6, transcendentals=0
        ),
        name="up",
    )(x, distant(gate_weight), distant(up_weight))


def act_kernel(acc_ref, x_ref, w_ref, act_ref):
    acc = raise_up(x_ref, w_ref, acc_ref[...])
    units = act_ref.shape[1]
    gated = acc[:, :units]
    act_ref[...] = (gated / (1.0 + jnp.exp(-gated)) * acc[:, units:]).astype(bf16)


def activate(acc, x, weight):
    slots = acc.shape[0]
    units = weight.shape[-1] // 2
    whole = pl.BlockSpec(memory_space=pltpu.VMEM)
    return pl.pallas_call(
        act_kernel,
        in_specs=[whole] * 3,
        out_specs=whole,
        out_shape=jax.ShapeDtypeStruct((slots, units), bf16),
        compiler_params=pltpu.CompilerParams(vmem_limit_bytes=VMEM),
        cost_estimate=pl.CostEstimate(
            flops=4 * slots * units * weight.shape[0] * weight.shape[1],
            bytes_accessed=6 * 10**6,
            transcendentals=slots * units,
        ),
        name="activate",
    )(acc, x, weight)


def cut_kernel(w_hbm, out_ref):
    pltpu.sync_copy(w_hbm.at[:, quarter_lanes(2, out_ref.shape[1])], out_ref)


def cut(down_weight):
    units, width = down_weight.shape
    return pl.pallas_call(
        cut_kernel,
        in_specs=[pl.BlockSpec(memory_space=pltpu.HBM)],
        out_specs=pl.BlockSpec(memory_space=pltpu.VMEM),
        out_shape=jax.ShapeDtypeStruct((units, width // PLANES), bf16),
        compiler_params=pltpu.CompilerParams(vmem_limit_bytes=VMEM),
        cost_estimate=pl.CostEstimate(flops=0, bytes_accessed=2 * 10**6, transcendentals=0),
        name="cut",
    )(distant(down_weight))


def down_kernel(a0, a1, a2, a3, own_hbm, w1, w2, w3, gates_ref, out_ref, w_ref, sems):
    acts = (a0, a1, a2, a3)
    z = lax.axis_index("tensor")
    units = a0.shape[1]
    width = out_ref.shape[1]
    lanes = pl.ds(pl.multiple_of(z * width, width), width)
    copies = [
        pltpu.make_async_copy(source, w_ref.at[n * units : (n + 1) * units], sems.at[n])
        for n, source in enumerate((own_hbm.at[:, lanes], w1, w2, w3))
    ]
    for copy in copies:
        copy.start()
    gate = gates_ref[:, 0:1] + gates_ref[:, 1:2]
    left = jnp.concatenate([act[...] for act in acts], axis=1)
    for copy in copies:
        copy.wait()
    block = 256
    for at in range(0, width, block):
        made = jnp.dot(left, w_ref[:, at : at + block], preferred_element_type=f32)
        out_ref[:, at : at + block] = (made * gate).astype(bf16)


def down(acts, own_weight, weights, gates):
    slots = acts[0].shape[0]
    units, width = weights[0].shape
    whole = pl.BlockSpec(memory_space=pltpu.VMEM)
    far = pl.BlockSpec(memory_space=pltpu.HBM)
    return pl.pallas_call(
        down_kernel,
        in_specs=[whole] * 4 + [far] * 4 + [whole],
        out_specs=whole,
        out_shape=jax.ShapeDtypeStruct((slots, width), bf16),
        scratch_shapes=[
            pltpu.VMEM((PLANES * units, width), bf16),
            pltpu.SemaphoreType.DMA((PLANES,)),
        ],
        compiler_params=pltpu.CompilerParams(vmem_limit_bytes=VMEM),
        cost_estimate=pl.CostEstimate(
            flops=8 * slots * units * width, bytes_accessed=6 * 10**6, transcendentals=0
        ),
        name="down",
    )(*acts, distant(own_weight), *[distant(weight) for weight in weights], gates)


def join_kernel(y_ref, received_ref, own_hbm, other_hbm, gates_ref, out_ref, x_ref, sems):
    half, width = out_ref.shape
    columns = own_hbm.shape[2] // (CHIPS // QUARTER)
    dp, z = lax.axis_index("dp"), lax.axis_index("tensor")
    core = dp % CORES
    step_here = dp // CORES % 2
    chips = QUARTER // 2
    near = pl.ds(z * QUARTER + step_here * chips, chips)
    rows = pl.ds(pl.multiple_of(core * PART, PART), PART)
    copies = [
        pltpu.make_async_copy(source.at[near, rows], x_ref.at[n], sems.at[n])
        for n, source in enumerate((own_hbm, other_hbm))
    ]
    for copy in copies:
        copy.start()
    both, homes = [], []
    for q in range(CHIPS // QUARTER):
        at = pl.ds(pl.multiple_of(q * CORES * PART + core * PART, PART), PART)
        both.append(y_ref[at, :].astype(f32) + received_ref[q * PART : (q + 1) * PART, :].astype(f32))
        homes.append(gates_ref[at, 2:3])
    total = jnp.concatenate(both, axis=0)
    home = jnp.concatenate(homes, axis=0)
    out_ref[...] = total.astype(bf16)
    for copy in copies:
        copy.wait()
    block = chips * CORES * columns
    flip = core == 1
    parts = []
    for chip in range(chips):
        mine = unpacked(x_ref[0, chip].astype(f32), columns)
        theirs = unpacked(x_ref[1, chip].astype(f32), columns)
        parts.append(jnp.where(flip, theirs, mine))
        parts.append(jnp.where(flip, mine, theirs))
    hidden = jnp.concatenate(parts, axis=1) * home
    for step in range(width // block):

        @pl.when(step_here == step)
        def _():
            at = slice(step * block, (step + 1) * block)
            out_ref[:, at] = (total[:, at] + hidden).astype(bf16)


def join(y, received, own, other, gates):
    whole = pl.BlockSpec(memory_space=pltpu.VMEM)
    far = pl.BlockSpec(memory_space=pltpu.HBM)
    return pl.pallas_call(
        join_kernel,
        in_specs=[whole, whole, far, far, whole],
        out_specs=whole,
        out_shape=jax.ShapeDtypeStruct(received.shape, bf16),
        scratch_shapes=[
            pltpu.VMEM((2, QUARTER // 2, PART, own.shape[2]), bf16),
            pltpu.SemaphoreType.DMA((2,)),
        ],
        compiler_params=pltpu.CompilerParams(vmem_limit_bytes=VMEM),
        cost_estimate=pl.CostEstimate(flops=10**6, bytes_accessed=2 * 10**6, transcendentals=0),
        name="join",
    )(y, received, own, other, gates)


def around(value, x_core):
    return [value] + [move_ring(value, by, x_core) for by in (1, 3, 2)]


def local(
    residual,
    query_latent,
    query_rope,
    cache_latent,
    cache_rope,
    lengths,
    value_up,
    out_proj,
    gate_proj,
    up_proj,
    down_proj,
    groups,
    expert_picks,
    gate_levels,
):
    rows, model = residual.shape
    columns = out_proj.shape[1]
    dp = lax.axis_index("dp")
    z = lax.axis_index("tensor")
    core = dp % CORES
    chip = dp // CORES
    here_x, here_y = chip // SIDE, chip % SIDE

    quarter = model // PLANES
    opposite = move_z(cut(down_proj[0]), 2)

    flat, places_here, spread, *sent = attend(
        query_latent, query_rope, cache_latent, cache_rope, lengths, value_up, down_proj[0], residual, columns,
        (groups.T, expert_picks.T, gate_levels.T),
    )
    weighting = places_here == (jnp.arange(128) % CAP + 1).astype(bf16)
    weighting = weighting.astype(bf16)

    blocks = jnp.concatenate(around(flat, 0), axis=0)

    spread, blocks, opposite = lax.optimization_barrier((spread, blocks, opposite))
    residual_columns = lax.all_to_all(spread, "dp", split_axis=0, concat_axis=0, tiled=True)
    downs = [move_z(part, by) for part, by in zip(sent, (1, 3))] + [opposite]
    residual_columns = residual_columns.reshape(CHIPS, CORES, rows, columns)

    blocks = around(blocks, 1)
    blocks[3], downs[:2], residual_columns = lax.optimization_barrier(
        (blocks[3], downs[:2], residual_columns)
    )
    swapped = [move_core(block) for block in blocks]
    mine, places_mine, levels_mine = project(blocks, out_proj)
    theirs, places_theirs, levels_theirs = project(swapped, out_proj)
    mine, theirs = sum_z(mine, theirs)
    places, levels = (places_mine, places_theirs), (levels_mine, levels_theirs)

    far = jnp.arange(SIDE, dtype=jnp.int32)
    x_far = (here_x - far) % SIDE
    y_far = (here_y - far) % SIDE
    x_spot = (x_far ^ (x_far >> 1))[:, None]
    y_spot = (y_far ^ (y_far >> 1))[None, :]
    x_first = (y_spot * SIDE + x_spot).reshape(CHIPS)
    y_first = (x_spot * SIDE + y_spot).reshape(CHIPS)
    table = jnp.where(
        core == 0, jnp.concatenate([x_first, y_first]), jnp.concatenate([y_first, x_first])
    ).astype(jnp.int32)
    gates = gate_table(table, places, levels)
    outgoing = select(table, (mine, theirs), residual_columns, places)
    outgoing, gates = lax.optimization_barrier((outgoing, gates))

    own = chip_exchange(outgoing)
    other = move_core(own)
    gate_weight = gate_proj.reshape(CHIPS, CORES, columns, -1)
    up_weight = up_proj.reshape(CHIPS, CORES, columns, -1)
    acc, weight = up(own, gate_weight, up_weight)
    act = activate(acc, other, weight)
    acts = [act] + [move_z(act, by) for by in (1, 3, 2)]
    made = down(acts, down_proj[0], downs, gates)
    pieces = made.reshape(CHIPS // QUARTER, CORES, PART, quarter)
    theirs = lax.dynamic_index_in_dim(pieces, 1 - core, 1, keepdims=False)
    received = move_core(theirs.reshape(CHIPS * CAP, quarter))
    returning = join(made, received, own, other, gates)
    returning = returning.reshape(CHIPS, CAP, quarter)
    returning, weighting = lax.optimization_barrier((returning, weighting))

    returned = chip_exchange(returning).reshape(CHIPS * CAP, quarter)
    mixed = jnp.dot(weighting, returned, preferred_element_type=f32).astype(bf16)
    return spread_z(mixed).transpose(1, 0, 2).reshape(rows, model)


def solution(mesh):
    return jax.shard_map(
        local,
        mesh=mesh,
        in_specs=(
            P("dp", None),
            P("dp", "tensor", None),
            P("dp", "tensor", None),
            P("dp", None, None),
            P("dp", None, None),
            P("dp"),
            P("tensor", None, None),
            P("tensor", "dp"),
            P("dp", None, "tensor"),
            P("dp", None, "tensor"),
            P("dp", "tensor", None),
            P("dp", None),
            P("dp", None),
            P("dp", None),
        ),
        out_specs=P("dp", None),
        check_vma=False,
    )
```

```python
import jax
import jax.numpy as jnp
from jax import lax
from jax.experimental import pallas as pl
from jax.experimental.pallas import tpu as pltpu
from jax.sharding import PartitionSpec as P

SIDE = 4
CORES = 2
CHIPS = SIDE * SIDE
PLANES = 4
TOPG = 4
GROUPS = 8
EPG = 4
CAP = 8
QUARTER = 4
PART = QUARTER * CAP

score_scale = 192.0 ** (-0.5)
route_scale = 2.5
far_below = -1e30

f32 = jnp.float32
bf16 = jnp.bfloat16
VMEM = 28 * 1024 * 1024


def distant(value):
    return pltpu.with_memory_space_constraint(value, pltpu.HBM)


def dp_index(x, y, c):
    return (x * SIDE + y) * CORES + c


def place_pairs(place):
    return [
        (dp_index(x, y, c), dp_index(*place(x, y, c)))
        for x in range(SIDE)
        for y in range(SIDE)
        for c in range(CORES)
    ]


def move_core(value):
    return lax.ppermute(value, "dp", place_pairs(lambda x, y, c: (x, y, 1 - c)))


def move_ring(value, by, x_core):
    def place(x, y, c):
        return ((x + by) % SIDE, y, c) if c == x_core else (x, (y + by) % SIDE, c)

    return lax.ppermute(value, "dp", place_pairs(place))


def move_z(value, by):
    return lax.ppermute(value, "tensor", [(z, (z + by) % PLANES) for z in range(PLANES)])


def spread_z(value):
    copies = jnp.broadcast_to(value[None], (PLANES,) + value.shape)
    return lax.all_to_all(copies, "tensor", split_axis=0, concat_axis=0, tiled=True)


def sum_z(low, high):
    def add(block, mask):
        pairs = [(z, z ^ mask) for z in range(PLANES)]
        moved = lax.ppermute(block, "tensor", pairs)
        return (block.astype(f32) + moved.astype(f32)).astype(bf16)

    low, high = add(low, 1), add(high, 3)
    low, high = add(low, 3), add(high, 1)
    return low, high


def chip_exchange(value):
    groups = [[dp_index(x, y, c) for x in range(SIDE) for y in range(SIDE)] for c in range(CORES)]
    return lax.all_to_all(
        value, "dp", split_axis=0, concat_axis=0, axis_index_groups=groups, tiled=True
    )


DEPTH = 6


def this_core():
    return lax.axis_index("dp") % CORES


def quarter_lanes(by, width):
    z = lax.axis_index("tensor")
    return pl.ds(pl.multiple_of((z + by) % PLANES * width, width), width)


def upright(ref):
    rows = ref.shape[1]
    same = lax.broadcasted_iota(jnp.int32, (rows, rows), 0) == lax.broadcasted_iota(
        jnp.int32, (rows, rows), 1
    )
    turned = lax.dot_general(
        jnp.where(same, 1.0, 0.0).astype(bf16),
        ref[...].astype(f32).astype(bf16),
        (((1,), (1,)), ((), ())),
        preferred_element_type=f32,
    )
    return turned.astype(jnp.int32)


def route_tables(groups, picks, levels):
    rows = groups.shape[0]
    lane = lax.broadcasted_iota(jnp.int32, (rows, 128), 1)
    member = lane < 0
    for t in range(TOPG):
        member = member | (lane // 16 == groups[:, t : t + 1])
    below = lax.broadcasted_iota(jnp.int32, (rows, rows), 0) >= lax.broadcasted_iota(
        jnp.int32, (rows, rows), 1
    )
    counted = jnp.dot(
        jnp.where(below, 1.0, 0.0).astype(bf16),
        jnp.where(member, 1.0, 0.0).astype(bf16),
        preferred_element_type=f32,
    )
    places = jnp.where(member, counted, 0.0)
    table = jnp.where(lane - GROUPS * EPG == groups[:, :1], 1, 0)
    for k in range(picks.shape[1]):
        pick = picks[:, k : k + 1]
        group = jnp.zeros_like(pick)
        for t in range(TOPG):
            group = jnp.where(pick // EPG == t, groups[:, t : t + 1], group)
        table = jnp.where(lane == group * EPG + pick % EPG, levels[:, k : k + 1], table)
    return places.astype(bf16), table.astype(f32).astype(bf16)


def attend_kernel(
    lengths, q_ref, qr_ref, k_hbm, r_hbm, vu_hbm, dw_hbm, res_ref, groups_ref, picks_ref, levels_ref,
    out_ref, places_ref, spread_ref, cut_1, cut_3,
    k_ref, r_ref, mix_ref, vu_ref, cut_ref, sems, cut_sems, vu_sem,
):
    rows, heads, lat = q_ref.shape
    width = vu_ref.shape[2]
    cuts = (cut_1, cut_3)
    vu_copy = pltpu.make_async_copy(vu_hbm, vu_ref, vu_sem)

    def copies(row, slot):
        return (
            pltpu.make_async_copy(k_hbm.at[row], k_ref.at[slot], sems.at[0, slot]),
            pltpu.make_async_copy(r_hbm.at[row], r_ref.at[slot], sems.at[1, slot]),
        )

    entering, leaving = [], []
    for n, by in enumerate((1, 3)):
        lanes = quarter_lanes(by, cut_ref.shape[2])
        entering.append(pltpu.make_async_copy(dw_hbm.at[:, lanes], cut_ref.at[n], cut_sems.at[0, n]))
        leaving.append(pltpu.make_async_copy(cut_ref.at[n], cuts[n], cut_sems.at[1, n]))
    for row in range(DEPTH):
        for copy in copies(row, row):
            copy.start()
    for copy in entering:
        copy.start()
    vu_copy.start()

    columns = spread_ref.shape[2]
    for j in range(spread_ref.shape[0]):
        spread_ref[j] = res_ref[:, j * columns : (j + 1) * columns]
    places, levels = route_tables(upright(groups_ref), upright(picks_ref), upright(levels_ref))
    places_ref[...] = places
    out_ref[:, heads * width : heads * width + 128] = places
    out_ref[:, heads * width + 128 :] = levels

    def scores_of(row, slot):
        scores = lax.dot_general(
            q_ref[row], k_ref[slot], (((1,), (1,)), ((), ())), preferred_element_type=f32
        )
        return scores + jnp.dot(qr_ref[row], r_ref[slot], preferred_element_type=f32)

    def weights_of(scores, row):
        scores = scores * score_scale
        place = lax.broadcasted_iota(jnp.int32, scores.shape, 1)
        scores = jnp.where(place < lengths[row], scores, far_below)
        highest = jnp.max(scores, axis=1, keepdims=True)
        raised = jnp.exp(scores - highest)
        return (raised * (1.0 / jnp.sum(raised, axis=1, keepdims=True))).astype(bf16)

    def finish(scores, row, slot):
        mix = jnp.dot(weights_of(scores, row), k_ref[slot], preferred_element_type=f32)
        at = pl.ds(row * heads, heads)
        for j in range(mix_ref.shape[0]):
            mix_ref[j, at, :] = mix[:, j * 128 : (j + 1) * 128]

    def wait(row, slot):
        for copy in copies(row, slot):
            copy.wait()

    scored, weighed = {}, {}
    for row in range(rows + 2):
        if row < rows:
            wait(row, row % DEPTH)
            scored[row] = scores_of(row, row % DEPTH)
        if 0 <= row - 1 < rows:
            weighed[row - 1] = weights_of(scored.pop(row - 1), row - 1)
        if row >= 2:
            done = row - 2
            mix = jnp.dot(weighed.pop(done), k_ref[done % DEPTH], preferred_element_type=f32)
            at = pl.ds(done * heads, heads)
            for j in range(mix_ref.shape[0]):
                mix_ref[j, at, :] = mix[:, j * 128 : (j + 1) * 128]
            if done + DEPTH < rows:
                for copy in copies(done + DEPTH, done % DEPTH):
                    copy.start()
        if row == DEPTH:
            for n, copy in enumerate(entering):
                copy.wait()
                leaving[n].start()
    vu_copy.wait()
    for h in range(heads):
        left = [mix_ref[j, pl.ds(h, rows, stride=heads), :] for j in range(mix_ref.shape[0])]
        left = jnp.concatenate(left, axis=1).astype(bf16)
        out_ref[:, h * width : (h + 1) * width] = jnp.dot(
            left, vu_ref[h], preferred_element_type=f32
        ).astype(bf16)
    for copy in leaving:
        copy.wait()


def attend(
    query_latent, query_rope, cache_latent, cache_rope, lengths, value_up, down_weight, residual, columns, routing
):
    rows, heads, lat = query_latent.shape
    rope = query_rope.shape[2]
    positions = cache_latent.shape[1]
    width = value_up.shape[2]
    units, model = down_weight.shape
    whole = pl.BlockSpec(memory_space=pltpu.VMEM)
    small = pl.BlockSpec(memory_space=pltpu.SMEM)
    far = pl.BlockSpec(memory_space=pltpu.HBM)
    return pl.pallas_call(
        attend_kernel,
        in_specs=[small, whole, whole] + [far] * 4 + [whole] * 4,
        out_specs=(whole,) * 3 + (far,) * 2,
        out_shape=(
            jax.ShapeDtypeStruct((rows, heads * width + 2 * 128), bf16),
            jax.ShapeDtypeStruct((rows, 128), bf16),
            jax.ShapeDtypeStruct((residual.shape[1] // columns, rows, columns), bf16),
        )
        + (jax.ShapeDtypeStruct((units, model // PLANES), bf16),) * 2,
        scratch_shapes=[
            pltpu.VMEM((DEPTH, positions, lat), bf16),
            pltpu.VMEM((DEPTH, rope, positions), bf16),
            pltpu.VMEM((lat // 128, (rows + 1) * heads, 128), f32),
            pltpu.VMEM((heads, lat, width), bf16),
            pltpu.VMEM((2, units, model // PLANES), bf16),
            pltpu.SemaphoreType.DMA((2, DEPTH)),
            pltpu.SemaphoreType.DMA((2, 2)),
            pltpu.SemaphoreType.DMA,
        ],
        compiler_params=pltpu.CompilerParams(vmem_limit_bytes=VMEM),
        cost_estimate=pl.CostEstimate(
            flops=4 * rows * heads * positions * lat,
            bytes_accessed=2 * rows * positions * (lat + rope),
            transcendentals=rows * heads * positions,
        ),
        name="attend",
    )(
        lengths, query_latent, query_rope, distant(cache_latent), distant(cache_rope), distant(value_up),
        distant(down_weight), residual, *routing,
    )


def project_kernel(*refs):
    blocks, w_ref = refs[:SIDE], refs[SIDE]
    out_ref, places_ref, levels_ref, b_ref, sems = refs[SIDE + 1 :]
    depth = w_ref.shape[1]
    moves = [
        pltpu.make_async_copy(block, b_ref.at[n], sems.at[n]) for n, block in enumerate(blocks)
    ]
    for move in moves:
        move.start()
    for move in moves:
        move.wait()
    blocks = [b_ref.at[n] for n in range(SIDE)]
    left = jnp.concatenate([block[:, :depth] for block in blocks])
    rows = out_ref.shape[1]
    for i, block in enumerate(blocks):
        for j in range(SIDE):
            at = slice(j * rows, (j + 1) * rows)
            places_ref[i * SIDE + j] = block[at, depth : depth + 128]
            levels_ref[i * SIDE + j] = block[at, depth + 128 :]
    made = lax.dot_general(left, w_ref[...], (((1,), (1,)), ((), ())), preferred_element_type=f32)
    made = made.astype(bf16)
    for n in range(CHIPS):
        out_ref[n] = made[n * rows : (n + 1) * rows]


def project(blocks, out_proj):
    columns = out_proj.shape[1]
    rows = blocks[0].shape[0] // SIDE
    whole = pl.BlockSpec(memory_space=pltpu.VMEM)
    far = pl.BlockSpec(memory_space=pltpu.HBM)
    table = pltpu.HBM((CHIPS, rows, 128), bf16)
    return pl.pallas_call(
        project_kernel,
        in_specs=[far] * SIDE + [whole],
        out_specs=(whole,) * 3,
        out_shape=(jax.ShapeDtypeStruct((CHIPS, rows, columns), bf16), table, table),
        scratch_shapes=[
            pltpu.VMEM((SIDE,) + blocks[0].shape, bf16),
            pltpu.SemaphoreType.DMA((SIDE,)),
        ],
        compiler_params=pltpu.CompilerParams(vmem_limit_bytes=VMEM),
        cost_estimate=pl.CostEstimate(flops=5 * 10**8, bytes_accessed=4 * 10**6, transcendentals=0),
        name="project",
    )(*blocks, out_proj.T)


def of_core(parity, table, chip, mine_ref, other_ref):
    mine = mine_ref[table[chip]].astype(f32)
    other = other_ref[table[CHIPS + chip]].astype(f32)
    return jnp.where(this_core() == parity, mine, other)


def slot_masks(mark, rows):
    lane = lax.broadcasted_iota(jnp.int32, (2 * rows, 128), 1)
    wanted = (lane % CAP + 1).astype(f32)
    second = lax.broadcasted_iota(jnp.int32, (2 * rows, 128), 0) >= rows
    right_half = (lane % (2 * CAP) >= CAP) == second
    return jnp.where((mark == wanted) & right_half, 1.0, 0.0).astype(bf16)


def gate_kernel(table, places_ref, places_other, levels_ref, levels_other, out_ref, made_ref):
    dp = lax.axis_index("dp")
    group = dp // EPG
    rows = places_ref.shape[1]
    lane = lax.broadcasted_iota(jnp.int32, (2 * rows, 128), 1)
    for quarter in range(CHIPS // QUARTER):
        for parity in range(CORES):
            for pair in range(QUARTER // 2):
                chips = (quarter * QUARTER + 2 * pair, quarter * QUARTER + 2 * pair + 1)
                mark = jnp.concatenate(
                    [of_core(parity, table, chip, places_ref, places_other) for chip in chips]
                )
                level = jnp.concatenate(
                    [of_core(parity, table, chip, levels_ref, levels_other) for chip in chips]
                )
                total = jnp.sum(jnp.where(lane < GROUPS * EPG, level, 0.0), axis=1, keepdims=True)
                mine = jnp.sum(jnp.where(lane == dp, level, 0.0), axis=1, keepdims=True)
                home = jnp.sum(
                    jnp.where(lane == GROUPS * EPG + group, level, 0.0), axis=1, keepdims=True
                )
                gate = route_scale * mine / total
                high = gate.astype(bf16).astype(f32)
                values = jnp.where(lane == 0, high, jnp.where(lane == 1, gate - high, 0.0))
                values = jnp.where(lane == 2, home, values).astype(bf16)
                made_ref[...] = lax.dot_general(
                    slot_masks(mark, rows), values, (((0,), (0,)), ((), ())),
                    preferred_element_type=f32,
                )
                to = quarter * CORES * PART + parity * PART + pair * 2 * CAP
                out_ref[to : to + 2 * CAP] = made_ref[
                    pl.ds(pl.multiple_of(group * 2 * CAP, 2 * CAP), 2 * CAP)
                ]


def gate_table(table, places, levels):
    whole = pl.BlockSpec(memory_space=pltpu.VMEM)
    return pl.pallas_call(
        gate_kernel,
        in_specs=[pl.BlockSpec(memory_space=pltpu.SMEM)] + [whole] * 4,
        out_specs=whole,
        out_shape=jax.ShapeDtypeStruct((CHIPS * CORES * CAP, 128), f32),
        scratch_shapes=[pltpu.VMEM((128, 128), f32)],
        compiler_params=pltpu.CompilerParams(vmem_limit_bytes=VMEM),
        cost_estimate=pl.CostEstimate(flops=10**8, bytes_accessed=10**6, transcendentals=0),
        name="gate_table",
    )(table, *[distant(value) for value in (*places, *levels)])


def select_kernel(table, sums_ref, sums_other, res_ref, places_ref, places_other, out_ref):
    rows = res_ref.shape[2]

    for parity in range(CORES):
        for pair in range(QUARTER // 2):
            quarters = []
            for quarter in range(CHIPS // QUARTER):
                parts = []
                marks = []
                for chip in (quarter * QUARTER + 2 * pair, quarter * QUARTER + 2 * pair + 1):
                    attention = of_core(parity, table, chip, sums_ref, sums_other)
                    parts.append((res_ref[chip, parity].astype(f32) + attention).astype(bf16))
                    marks.append(of_core(parity, table, chip, places_ref, places_other))
                hidden = jnp.concatenate(parts, axis=0)
                mark = jnp.concatenate(marks, axis=0)
                pick = slot_masks(mark, rows)
                quarters.append(
                    lax.dot_general(
                        pick, hidden, (((0,), (0,)), ((), ())), preferred_element_type=f32
                    )
                )
            chosen = jnp.concatenate(quarters, axis=1).astype(bf16)
            at = parity * PART + pair * 2 * CAP
            for group in range(GROUPS):
                block = chosen[group * 2 * CAP : (group + 1) * 2 * CAP]
                out_ref[2 * group, at : at + 2 * CAP, :] = block
                out_ref[2 * group + 1, at : at + 2 * CAP, :] = block


def select(table, parts, residual, places):
    columns = residual.shape[-1]
    whole = pl.BlockSpec(memory_space=pltpu.VMEM)
    return pl.pallas_call(
        select_kernel,
        in_specs=[pl.BlockSpec(memory_space=pltpu.SMEM)] + [whole] * 5,
        out_specs=whole,
        out_shape=jax.ShapeDtypeStruct(
            (CHIPS, CORES * PART, CHIPS // QUARTER * columns), bf16
        ),
        compiler_params=pltpu.CompilerParams(vmem_limit_bytes=VMEM),
        cost_estimate=pl.CostEstimate(flops=10**9, bytes_accessed=6 * 10**6, transcendentals=0),
        name="select",
    )(table, *parts, distant(residual), *[distant(value) for value in places])


def unpacked(block, columns):
    parts = [block[:, q * columns : (q + 1) * columns] for q in range(CHIPS // QUARTER)]
    return jnp.concatenate(parts, axis=0)


def weight_copies(gw_hbm, uw_hbm, w_ref, sems, core):
    units = gw_hbm.shape[-1]
    span = CHIPS // QUARTER
    copies = []
    for part in range(QUARTER):
        chips = pl.ds(part * span, span)
        for n, source in enumerate((gw_hbm, uw_hbm)):
            lanes = slice(n * units, (n + 1) * units)
            copies.append(
                pltpu.make_async_copy(
                    source.at[chips, core], w_ref.at[chips, :, lanes], sems.at[part, n]
                )
            )
    return copies


def raise_up(x_ref, w_ref, acc, copies=None):
    span = CHIPS // QUARTER
    for chip in range(CHIPS):
        if copies is not None and chip % span == 0:
            copies[chip // span * 2].wait()
            copies[chip // span * 2 + 1].wait()
        acc = acc + jnp.dot(
            unpacked(x_ref[chip], w_ref.shape[1]), w_ref[chip], preferred_element_type=f32
        )
    return acc


def up_kernel(x_ref, gw_hbm, uw_hbm, acc_ref, next_ref, w_ref, sems, next_sems):
    core = this_core()
    copies = weight_copies(gw_hbm, uw_hbm, w_ref, sems, core)
    following = weight_copies(gw_hbm, uw_hbm, next_ref, next_sems, 1 - core)
    for copy in copies + following:
        copy.start()
    acc_ref[...] = raise_up(x_ref, w_ref, jnp.zeros(acc_ref.shape, f32), copies)
    for copy in following:
        copy.wait()


def up(x, gate_weight, up_weight):
    columns, units = gate_weight.shape[2:]
    slots = x.shape[1] * CHIPS // QUARTER
    whole = pl.BlockSpec(memory_space=pltpu.VMEM)
    far = pl.BlockSpec(memory_space=pltpu.HBM)
    return pl.pallas_call(
        up_kernel,
        in_specs=[whole, far, far],
        out_specs=(whole, whole),
        out_shape=(
            jax.ShapeDtypeStruct((slots, 2 * units), f32),
            pltpu.VMEM((CHIPS, columns, 2 * units), bf16),
        ),
        scratch_shapes=[
            pltpu.VMEM((CHIPS, columns, 2 * units), bf16),
            pltpu.SemaphoreType.DMA((QUARTER, 2)),
            pltpu.SemaphoreType.DMA((QUARTER, 2)),
        ],
        compiler_params=pltpu.CompilerParams(vmem_limit_bytes=VMEM),
        cost_estimate=pl.CostEstimate(
            flops=4 * CHIPS * slots * columns * units, bytes_accessed=9 * 10**6, transcendentals=0
        ),
        name="up",
    )(x, distant(gate_weight), distant(up_weight))


def act_kernel(acc_ref, x_ref, w_ref, act_ref):
    acc = raise_up(x_ref, w_ref, acc_ref[...])
    units = act_ref.shape[1]
    gated = acc[:, :units]
    act_ref[...] = (gated / (1.0 + jnp.exp(-gated)) * acc[:, units:]).astype(bf16)


def activate(acc, x, weight):
    slots = acc.shape[0]
    units = weight.shape[-1] // 2
    whole = pl.BlockSpec(memory_space=pltpu.VMEM)
    return pl.pallas_call(
        act_kernel,
        in_specs=[whole] * 3,
        out_specs=whole,
        out_shape=jax.ShapeDtypeStruct((slots, units), bf16),
        compiler_params=pltpu.CompilerParams(vmem_limit_bytes=VMEM),
        cost_estimate=pl.CostEstimate(
            flops=4 * slots * units * weight.shape[0] * weight.shape[1],
            bytes_accessed=6 * 10**6,
            transcendentals=slots * units,
        ),
        name="activate",
    )(acc, x, weight)


def cut_kernel(w_hbm, out_ref):
    pltpu.sync_copy(w_hbm.at[:, quarter_lanes(2, out_ref.shape[1])], out_ref)


def cut(down_weight):
    units, width = down_weight.shape
    return pl.pallas_call(
        cut_kernel,
        in_specs=[pl.BlockSpec(memory_space=pltpu.HBM)],
        out_specs=pl.BlockSpec(memory_space=pltpu.VMEM),
        out_shape=jax.ShapeDtypeStruct((units, width // PLANES), bf16),
        compiler_params=pltpu.CompilerParams(vmem_limit_bytes=VMEM),
        cost_estimate=pl.CostEstimate(flops=0, bytes_accessed=2 * 10**6, transcendentals=0),
        name="cut",
    )(distant(down_weight))


def down_kernel(a0, a1, a2, a3, own_hbm, w1, w2, w3, gates_ref, out_ref, w_ref, sems):
    acts = (a0, a1, a2, a3)
    z = lax.axis_index("tensor")
    units = a0.shape[1]
    width = out_ref.shape[1]
    lanes = pl.ds(pl.multiple_of(z * width, width), width)
    copies = [
        pltpu.make_async_copy(source, w_ref.at[n * units : (n + 1) * units], sems.at[n])
        for n, source in enumerate((own_hbm.at[:, lanes], w1, w2, w3))
    ]
    for copy in copies:
        copy.start()
    gate = gates_ref[:, 0:1] + gates_ref[:, 1:2]
    left = jnp.concatenate([act[...] for act in acts], axis=1)
    for copy in copies:
        copy.wait()
    block = 256
    for at in range(0, width, block):
        made = jnp.dot(left, w_ref[:, at : at + block], preferred_element_type=f32)
        out_ref[:, at : at + block] = (made * gate).astype(bf16)


def down(acts, own_weight, weights, gates):
    slots = acts[0].shape[0]
    units, width = weights[0].shape
    whole = pl.BlockSpec(memory_space=pltpu.VMEM)
    far = pl.BlockSpec(memory_space=pltpu.HBM)
    return pl.pallas_call(
        down_kernel,
        in_specs=[whole] * 4 + [far] * 4 + [whole],
        out_specs=whole,
        out_shape=jax.ShapeDtypeStruct((slots, width), bf16),
        scratch_shapes=[
            pltpu.VMEM((PLANES * units, width), bf16),
            pltpu.SemaphoreType.DMA((PLANES,)),
        ],
        compiler_params=pltpu.CompilerParams(vmem_limit_bytes=VMEM),
        cost_estimate=pl.CostEstimate(
            flops=8 * slots * units * width, bytes_accessed=6 * 10**6, transcendentals=0
        ),
        name="down",
    )(*acts, distant(own_weight), *[distant(weight) for weight in weights], gates)


def join_kernel(y_ref, received_ref, own_hbm, other_hbm, gates_ref, out_ref, x_ref, sems):
    half, width = out_ref.shape
    columns = own_hbm.shape[2] // (CHIPS // QUARTER)
    dp, z = lax.axis_index("dp"), lax.axis_index("tensor")
    core = dp % CORES
    step_here = dp // CORES % 2
    chips = QUARTER // 2
    near = pl.ds(z * QUARTER + step_here * chips, chips)
    rows = pl.ds(pl.multiple_of(core * PART, PART), PART)
    copies = [
        pltpu.make_async_copy(source.at[near, rows], x_ref.at[n], sems.at[n])
        for n, source in enumerate((own_hbm, other_hbm))
    ]
    for copy in copies:
        copy.start()
    both, homes = [], []
    for q in range(CHIPS // QUARTER):
        at = pl.ds(pl.multiple_of(q * CORES * PART + core * PART, PART), PART)
        both.append(y_ref[at, :].astype(f32) + received_ref[q * PART : (q + 1) * PART, :].astype(f32))
        homes.append(gates_ref[at, 2:3])
    total = jnp.concatenate(both, axis=0)
    home = jnp.concatenate(homes, axis=0)
    out_ref[...] = total.astype(bf16)
    for copy in copies:
        copy.wait()
    block = chips * CORES * columns
    flip = core == 1
    parts = []
    for chip in range(chips):
        mine = unpacked(x_ref[0, chip].astype(f32), columns)
        theirs = unpacked(x_ref[1, chip].astype(f32), columns)
        parts.append(jnp.where(flip, theirs, mine))
        parts.append(jnp.where(flip, mine, theirs))
    hidden = jnp.concatenate(parts, axis=1) * home
    for step in range(width // block):

        @pl.when(step_here == step)
        def _():
            at = slice(step * block, (step + 1) * block)
            out_ref[:, at] = (total[:, at] + hidden).astype(bf16)


def join(y, received, own, other, gates):
    whole = pl.BlockSpec(memory_space=pltpu.VMEM)
    far = pl.BlockSpec(memory_space=pltpu.HBM)
    return pl.pallas_call(
        join_kernel,
        in_specs=[whole, whole, far, far, whole],
        out_specs=whole,
        out_shape=jax.ShapeDtypeStruct(received.shape, bf16),
        scratch_shapes=[
            pltpu.VMEM((2, QUARTER // 2, PART, own.shape[2]), bf16),
            pltpu.SemaphoreType.DMA((2,)),
        ],
        compiler_params=pltpu.CompilerParams(vmem_limit_bytes=VMEM),
        cost_estimate=pl.CostEstimate(flops=10**6, bytes_accessed=2 * 10**6, transcendentals=0),
        name="join",
    )(y, received, own, other, gates)


def around(value, x_core):
    return [value] + [move_ring(value, by, x_core) for by in (1, 3, 2)]


def local(
    residual,
    query_latent,
    query_rope,
    cache_latent,
    cache_rope,
    lengths,
    value_up,
    out_proj,
    gate_proj,
    up_proj,
    down_proj,
    groups,
    expert_picks,
    gate_levels,
):
    rows, model = residual.shape
    columns = out_proj.shape[1]
    dp = lax.axis_index("dp")
    z = lax.axis_index("tensor")
    core = dp % CORES
    chip = dp // CORES
    here_x, here_y = chip // SIDE, chip % SIDE

    quarter = model // PLANES
    opposite = move_z(cut(down_proj[0]), 2)

    flat, places_here, spread, *sent = attend(
        query_latent, query_rope, cache_latent, cache_rope, lengths, value_up, down_proj[0], residual, columns,
        (groups.T, expert_picks.T, gate_levels.T),
    )
    weighting = places_here == (jnp.arange(128) % CAP + 1).astype(bf16)
    weighting = weighting.astype(bf16)

    blocks = jnp.concatenate(around(flat, 0), axis=0)

    spread, blocks, opposite = lax.optimization_barrier((spread, blocks, opposite))
    residual_columns = lax.all_to_all(spread, "dp", split_axis=0, concat_axis=0, tiled=True)
    downs = [move_z(part, by) for part, by in zip(sent, (1, 3))] + [opposite]
    residual_columns = residual_columns.reshape(CHIPS, CORES, rows, columns)

    blocks = around(blocks, 1)
    blocks[3], downs[:2], residual_columns = lax.optimization_barrier(
        (blocks[3], downs[:2], residual_columns)
    )
    swapped = [move_core(block) for block in blocks]
    mine, places_mine, levels_mine = project(blocks, out_proj)
    theirs, places_theirs, levels_theirs = project(swapped, out_proj)
    mine, theirs = sum_z(mine, theirs)
    places, levels = (places_mine, places_theirs), (levels_mine, levels_theirs)

    far = jnp.arange(SIDE, dtype=jnp.int32)
    x_far = (here_x - far) % SIDE
    y_far = (here_y - far) % SIDE
    x_spot = (x_far ^ (x_far >> 1))[:, None]
    y_spot = (y_far ^ (y_far >> 1))[None, :]
    x_first = (y_spot * SIDE + x_spot).reshape(CHIPS)
    y_first = (x_spot * SIDE + y_spot).reshape(CHIPS)
    table = jnp.where(
        core == 0, jnp.concatenate([x_first, y_first]), jnp.concatenate([y_first, x_first])
    ).astype(jnp.int32)
    gates = gate_table(table, places, levels)
    outgoing = select(table, (mine, theirs), residual_columns, places)
    outgoing, gates = lax.optimization_barrier((outgoing, gates))

    own = chip_exchange(outgoing)
    other = move_core(own)
    gate_weight = gate_proj.reshape(CHIPS, CORES, columns, -1)
    up_weight = up_proj.reshape(CHIPS, CORES, columns, -1)
    acc, weight = up(own, gate_weight, up_weight)
    act = activate(acc, other, weight)
    acts = [act] + [move_z(act, by) for by in (1, 3, 2)]
    made = down(acts, down_proj[0], downs, gates)
    pieces = made.reshape(CHIPS // QUARTER, CORES, PART, quarter)
    theirs = lax.dynamic_index_in_dim(pieces, 1 - core, 1, keepdims=False)
    received = move_core(theirs.reshape(CHIPS * CAP, quarter))
    returning = join(made, received, own, other, gates)
    returning = returning.reshape(CHIPS, CAP, quarter)
    returning, weighting = lax.optimization_barrier((returning, weighting))

    returned = chip_exchange(returning).reshape(CHIPS * CAP, quarter)
    mixed = jnp.dot(weighting, returned, preferred_element_type=f32).astype(bf16)
    return spread_z(mixed).transpose(1, 0, 2).reshape(rows, model)


def solution(mesh):
    return jax.shard_map(
        local,
        mesh=mesh,
        in_specs=(
            P("dp", None),
            P("dp", "tensor", None),
            P("dp", "tensor", None),
            P("dp", None, None),
            P("dp", None, None),
            P("dp"),
            P("tensor", None, None),
            P("tensor", "dp"),
            P("dp", None, "tensor"),
            P("dp", None, "tensor"),
            P("dp", "tensor", None),
            P("dp", None),
            P("dp", None),
            P("dp", None),
        ),
        out_specs=P("dp", None),
        check_vma=False,
    )
```
